32 devices in a mesh: seq: 8 (over z, y), chan: 4 (over x, core).
Axes of the slice: x: 2, y: 2, z: 4, core: 2. Of those that a mesh axis runs over, the one named last changes fastest.
Arguments:
- signal: bfloat16 [2048, 2048], P('seq', 'chan'), may hold values from -6 to 6
- gate_rows: bfloat16 [2048, 2048], P('seq', 'chan'), may hold values from -60 to 60
- skip_gain: float32 [2048], P('chan'), may hold values from 0.5 to 1.5
- filter_taps: bfloat16 [2048, 16], P(None, 'chan'), may hold values from -2 to 2
- queries: bfloat16 [2048, 2048], P('seq', 'chan'), may hold values from -6 to 6
- key_rows: bfloat16 [2048, 2048], P('seq', 'chan'), may hold values from -6 to 6
Outputs:
- conv_mixed: bfloat16 [2048, 2048], P('seq', 'chan')
- attended: bfloat16 [32, 1024, 128], P(('chan', 'seq'))
The draws below stay inside these ranges and needn't reach their ends.
All inputs are finite; a program needn't handle non-finite values.
Results may differ from the reference program's by a relative error of at most 0.0061.
Values may be sent and summed in bfloat16 or wider, within the bound.
No kernel may reach another device: no remote copies, remote signals or barrier semaphores. Data moves between devices by JAX's collectives and lax.ppermute only.
A program may use at most 128 MiB of HBM per device.

```python
import math
import jax
import jax.numpy as jnp
from jax import lax

HALF_HEADS = 16
HD = 128
DW = 2048
SEQUENCE_LENGTH = 2048
QB = 2
QROWS = 128
QLEN = 1024
N_SEQ = 8


def draw_queries(key, part):
    base = jax.random.fold_in(key, 1)
    drawn = jnp.clip(jax.random.normal(base, (SEQUENCE_LENGTH, DW), jnp.float32), -4.0, 4.0)
    return drawn.astype(jnp.bfloat16)


def draw_key_rows(key, part):
    base = jax.random.fold_in(key, 2)
    drawn = jnp.clip(jax.random.normal(base, (SEQUENCE_LENGTH, DW), jnp.float32), -4.0, 4.0)
    return drawn.astype(jnp.bfloat16)


def draw_gate_rows(key, part):
    base = jax.random.fold_in(key, 4)
    key_collection = jax.random.split(base, 3)
    ramp = jnp.exp(math.log(10.0) * jnp.arange(DW, dtype=jnp.float32) / max(DW - 1, 1)) / math.sqrt(10.0)
    columns = ramp * jax.random.uniform(key_collection[1], (DW,), jnp.float32, 0.7, 1.4)
    row_scale = jnp.exp(jax.random.uniform(key_collection[2], (SEQUENCE_LENGTH, 1), jnp.float32, 0.0, math.log(10.0))) / math.sqrt(10.0)
    drawn = jnp.clip(jax.random.normal(key_collection[0], (SEQUENCE_LENGTH, DW), jnp.float32), -4.0, 4.0)
    return (drawn * row_scale * columns[None, :]).astype(jnp.bfloat16)


def draw_filter_taps(key, part):
    base = jax.random.fold_in(key, 5)
    key_collection = jax.random.split(base, 6)
    slow_share = 0.6
    slow_heads = jax.random.uniform(key_collection[0], (HALF_HEADS,), jnp.float32) < slow_share
    tau_slow = jnp.exp(jax.random.uniform(key_collection[1], (HALF_HEADS,), jnp.float32, math.log(SEQUENCE_LENGTH / 2.0), math.log(8.0 * SEQUENCE_LENGTH)))
    tau_fast = jnp.exp(jax.random.uniform(key_collection[2], (HALF_HEADS,), jnp.float32, math.log(20.0), math.log(60.0)))
    decay_len = jnp.where(slow_heads, tau_slow, tau_fast)
    delay_index = jnp.arange(SEQUENCE_LENGTH, dtype=jnp.float32)[:, None]
    spike_positions = jax.random.randint(key_collection[3], (4, HALF_HEADS), 0, SEQUENCE_LENGTH).astype(jnp.float32)
    spike_keep_mask = jax.random.uniform(key_collection[4], (4, HALF_HEADS), jnp.float32, 0.5, 0.8)
    spike_values = jnp.prod(jnp.where(delay_index[None, :, :] >= spike_positions[:, None, :], spike_keep_mask[:, None, :], 1.0), axis=0)
    decay_ratio = jnp.exp(-2.0 / decay_len)
    energy = (1.0 - decay_ratio ** SEQUENCE_LENGTH) / (1.0 - decay_ratio)
    decay_profile = jnp.exp(-delay_index / decay_len[None, :]) / jnp.sqrt(energy)[None, :]
    noisy_filter_taps = jnp.clip(jax.random.normal(key_collection[5], (SEQUENCE_LENGTH, HALF_HEADS), jnp.float32), -4.0, 4.0)
    return (noisy_filter_taps * decay_profile * spike_values).astype(jnp.bfloat16)


def steps_of(rng, dims, cuts, low, high):
    gain, own = 1.0, jax.random.fold_in(rng, 6)
    for dim, blocks in cuts:
        steps = jnp.exp(jax.random.uniform(jax.random.fold_in(own, dim), (blocks,), jnp.float32, low / len(cuts), high / len(cuts)))
        gain = gain * jnp.repeat(steps, dims[dim] // blocks).reshape([-1 if axis == dim else 1 for axis in range(len(dims))])
    return gain


def gaussian(stream_key, shape, width, reach, pieces=(), kind=jnp.bfloat16):
    values = jax.random.normal(stream_key, shape, jnp.float32) * width
    if len(pieces) > 0:
        values = steps_of(stream_key, shape, pieces, -0.22, 0.18) * values
    return jnp.clip(values, min=-reach, max=reach).astype(kind)


def setup_inputs(seed: int = 0) -> dict:
    seeds = jax.random.split(jax.random.key(seed), 7)
    return {
        "signal": gaussian(seeds[0], (SEQUENCE_LENGTH, DW), 1.0, 6.0, ((0, 8), (1, 4))),
        "gate_rows": draw_gate_rows(jax.random.fold_in(seeds[6], 71), 0),
        "skip_gain": jnp.clip(0.5 + 1.0 * jax.random.uniform(seeds[2], (DW,), jnp.float32) ** steps_of(seeds[2], (DW,), ((0, 4),), -0.2, 0.2), 0.5, 1.5),
        "filter_taps": draw_filter_taps(jax.random.fold_in(seeds[6], 71), 0),
        "queries": draw_queries(jax.random.fold_in(seeds[6], 71), 0),
        "key_rows": draw_key_rows(jax.random.fold_in(seeds[6], 71), 0),
    }


def reference(signal, gate_rows, skip_gain, filter_taps, queries, key_rows):
    length = SEQUENCE_LENGTH
    inputs = signal.astype(jnp.float32)
    channel_taps = jnp.repeat(filter_taps.astype(jnp.float32), HD, axis=1)
    spectrum = jnp.fft.rfft(inputs, 2 * length, axis=0) * jnp.fft.rfft(channel_taps, 2 * length, axis=0)
    conv_sum = jnp.fft.irfft(spectrum, 2 * length, axis=0)[:length].astype(jnp.float32)
    conv_mixed = (gate_rows.astype(jnp.float32) * (conv_sum + skip_gain[None, :] * inputs)).astype(jnp.bfloat16)
    widened = conv_mixed.astype(jnp.float32)
    inv_scale = lax.rsqrt(lax.optimization_barrier(jnp.sum(widened * widened, axis=1)) / DW + 1e-06)
    values = (widened * inv_scale[:, None]).astype(jnp.bfloat16)
    head_q = queries.reshape(length, HALF_HEADS, HD).transpose(1, 0, 2)
    head_k = key_rows.reshape(length, HALF_HEADS, HD).transpose(1, 0, 2)
    head_v = values.reshape(length, HALF_HEADS, HD).transpose(1, 0, 2)
    block_len = min(1024, length)
    score_scale = 1.0 / math.sqrt(HD)

    def one_head(operands):
        q_head, k_head, v_head = operands
        q_blocks = q_head.reshape(length // block_len, block_len, HD)
        firsts = jnp.arange(length // block_len, dtype=jnp.int32) * block_len

        def one_block(entry):
            q_rows, first_row = entry
            raw_scores = jnp.dot(q_rows, k_head.T, preferred_element_type=jnp.float32) * score_scale
            q_pos = first_row + jnp.arange(block_len, dtype=jnp.int32)
            k_pos = jnp.arange(length, dtype=jnp.int32)
            masked = jnp.where(k_pos[None, :] <= q_pos[:, None], raw_scores, -jnp.inf)
            peak = lax.optimization_barrier(jnp.max(masked, axis=1))
            exp_scores = jnp.exp(masked - peak[:, None])
            row_total = lax.optimization_barrier(jnp.sum(exp_scores, axis=1))
            weights = exp_scores.astype(jnp.bfloat16)
            summed = jnp.dot(weights, v_head, preferred_element_type=jnp.float32)
            return (summed / row_total[:, None]).astype(jnp.bfloat16)
        return lax.map(one_block, (q_blocks, firsts)).reshape(length, HD)
    heads_out = lax.map(one_head, (head_q, head_k, head_v))
    attended = heads_out.reshape(HALF_HEADS, N_SEQ, QB, QROWS, HD).transpose(0, 2, 1, 3, 4).reshape(HALF_HEADS * QB, QLEN, HD)
    return (conv_mixed, attended)
```

```python
import functools
import math

import jax
import jax.numpy as jnp
from jax import lax
from jax.experimental import pallas as pl
from jax.experimental.pallas import tpu as pltpu
from jax.sharding import PartitionSpec as P

BF16, F32 = jnp.bfloat16, jnp.float32
QUERY_BLOCK = 256
KEY_CHUNK = 512
VMEM_LIMIT = 56 * 1024 * 1024
NT = (((1,), (1,)), ((), ()))


def call(kernel, out_shape, flops=0, exps=0, moved=0, **options):
    return pl.pallas_call(
        kernel,
        out_shape=out_shape,
        compiler_params=pltpu.CompilerParams(vmem_limit_bytes=VMEM_LIMIT),
        cost_estimate=pl.CostEstimate(flops=flops, bytes_accessed=moved, transcendentals=exps),
        **options,
    )


def merge_rows(blocks):
    count, rows, columns = blocks.shape
    if blocks.dtype == BF16 and rows % 16:
        return blocks.astype(F32).reshape(count * rows, columns).astype(BF16)
    return blocks.reshape(count * rows, columns)


def loop(count, body, carry):
    if count <= 8:
        for index in range(count):
            carry = body(index, carry)
        return carry
    return lax.fori_loop(0, count, body, carry)


def split_kernel(signal_ref, gate_ref, sent_ref):
    count, _, rows, positions = sent_ref.shape
    for slot, ref in enumerate((signal_ref, gate_ref)):
        turned = ref[...].astype(F32).T
        sent_ref[:, slot] = turned.reshape(count, rows, positions).astype(BF16)


def pack_kernel(sets, query_ref, key_ref, sent_ref):
    count, _, rows, head_dim = sent_ref.shape
    for device in range(count):
        head, part = divmod(device, sets)
        for slot, ref in enumerate((query_ref, key_ref)):
            sent_ref[device, slot] = ref[
                part * rows : (part + 1) * rows, head * head_dim : (head + 1) * head_dim
            ]


def unsplit_kernel(got_ref, out_ref):
    out_ref[...] = merge_rows(got_ref[...].astype(F32)).T.astype(BF16)


def toeplitz_kernel(head_count_per, taps_ref, matrix_ref):
    block, length = matrix_ref.shape
    head = lax.axis_index("seq") // head_count_per
    taps = taps_ref[...].astype(F32)
    mine = lax.broadcasted_iota(jnp.int32, taps.shape, 0) == head
    row = jnp.sum(jnp.where(mine, taps, 0.0), axis=0, keepdims=True)
    rolled = pltpu.roll(jnp.broadcast_to(row, (block, length)), 0, 1, stride=1, stride_axis=0)
    source = lax.broadcasted_iota(jnp.int32, (block, block), 0)
    target = lax.broadcasted_iota(jnp.int32, (block, block), 1)
    matrix_ref[:, :block] = jnp.where(target >= source, rolled[:, :block], 0.0).astype(BF16)
    matrix_ref[:, block:] = rolled[:, block:].astype(BF16)


def conv_kernel(got_ref, matrix_ref, skip_ref, mixed_ref, squares_ref, total_ref):
    count, _, rows, block = got_ref.shape
    inputs = merge_rows(got_ref[:, 0])
    for lag in range(count):
        product = jnp.dot(
            inputs[: (count - lag) * rows],
            matrix_ref[:, lag * block : (lag + 1) * block],
            preferred_element_type=F32,
        )
        if lag == 0:
            total_ref[...] = product
        else:
            total_ref[lag * rows :] += product
    skip = skip_ref[...]
    sums = []
    for index in range(count):
        conv = total_ref[index * rows : (index + 1) * rows]
        direct = skip * got_ref[index, 0].astype(F32)
        mixed = (got_ref[index, 1].astype(F32) * (conv + direct)).astype(BF16)
        mixed_ref[index] = mixed
        widened = mixed.astype(F32)
        sums.append(jnp.sum(widened * widened, axis=0, keepdims=True))
    squares = jnp.concatenate(sums, axis=0).astype(BF16)
    for device in range(squares_ref.shape[0]):
        squares_ref[device] = squares


def weights_block(step, last, key_ref, query, sets, rows, scores_ref, weights_ref, total_ref):
    wide = query.shape[0]
    seq_block = sets * rows
    reach = wide // rows * seq_block
    chunk = min(KEY_CHUNK, reach)
    chunks = (step + 1) * reach // chunk
    head_dim = query.shape[1]
    factor = math.log2(math.e) / math.sqrt(head_dim)
    mine = lax.rem(lax.axis_index("seq"), sets)
    lane = step * wide + lax.broadcasted_iota(jnp.int32, (1, wide), 1)
    query_pos = lane // rows * seq_block + mine * rows + lax.rem(lane, rows)

    def score(index, peak):
        first = index * chunk
        part = key_ref[pl.ds(first, chunk), :]
        raw = lax.dot_general(part, query, NT, preferred_element_type=F32)
        if not isinstance(index, int) or first + chunk - 1 > step * reach:
            key_pos = first + lax.broadcasted_iota(jnp.int32, (chunk, 1), 0)
            raw = jnp.where(key_pos <= query_pos, raw, -jnp.inf)
        scores_ref[pl.ds(first, chunk), :] = raw
        return jnp.maximum(peak, jnp.max(raw, axis=0, keepdims=True))

    peak = loop(chunks, score, jnp.full((1, wide), -jnp.inf, F32))

    def weigh(index, total):
        first = index * chunk
        weights = jnp.exp2((scores_ref[pl.ds(first, chunk), :] - peak) * factor)
        weights_ref[pl.ds(first, chunk), :] = weights.astype(BF16)
        return total + jnp.sum(weights, axis=0, keepdims=True)

    total = loop(chunks, weigh, jnp.zeros((1, wide), F32))
    total_ref[...] = jnp.broadcast_to(total, total_ref.shape)


def weights_kernel(sets, gridded, got_ref, *refs):
    others, (weights_ref, total_ref, key_ref, query_ref, scores_ref) = refs[:-5], refs[-5:]
    count, _, rows, head_dim = got_ref.shape
    mine = lax.rem(lax.axis_index("seq"), sets)

    def assemble():
        query_ref[...] = merge_rows(got_ref[:, 0])
        for offset in range(sets):
            keys = got_ref[:, 1] if offset == 0 else others[offset - 1][...]
            place = lax.rem(mine + offset, sets)
            key_ref[:, pl.ds(place, 1)] = keys[:, None]

    steps = query_ref.shape[0] // QUERY_BLOCK
    keys = key_ref.reshape(count * sets * rows, head_dim)

    def block(step, weights, total):
        query = query_ref[step * QUERY_BLOCK : (step + 1) * QUERY_BLOCK]
        weights_block(step, steps - 1, keys, query, sets, rows, scores_ref, weights, total)

    if not gridded:
        assemble()
        for step in range(steps):
            block(step, weights_ref.at[step], total_ref.at[step])
        return
    pl.when(pl.program_id(0) == 0)(assemble)
    for step in range(steps):
        pl.when(pl.program_id(0) == step)(
            functools.partial(block, step, weights_ref.at[0], total_ref.at[0])
        )


def output_kernel(sets, width, gridded, squares_ref, weights_ref, total_ref, mixed_ref, *refs):
    others, (out_ref, wide_ref, values_ref) = refs[:-3], refs[-3:]
    count, rows, block = mixed_ref.shape
    mine = lax.rem(lax.axis_index("seq"), sets)
    steps = count * block // sets // QUERY_BLOCK
    reach = count * block // steps

    def norm():
        squares = jnp.sum(squares_ref[...].astype(F32), axis=0)
        inv_scale = lax.rsqrt(squares / width + 1e-06)
        for offset in range(sets):
            ref = mixed_ref if offset == 0 else others[offset - 1]
            place = lax.rem(mine + offset, sets)
            for index in range(count):
                part = ref[index].astype(F32) * inv_scale[index : index + 1]
                wide_ref[place, :, index * block : (index + 1) * block] = part
        for index in range(count):
            span = slice(index * block, (index + 1) * block)
            values_ref[:, span] = merge_rows(wide_ref[:, :, span]).astype(BF16)

    def attend(step, weights, total, out):
        keys = (step + 1) * reach
        summed = jnp.dot(values_ref[:, :keys], weights[:keys], preferred_element_type=F32)
        out[...] = (summed / total[:1]).T.astype(BF16)

    if not gridded:
        norm()
        for step in range(steps):
            rows_out = out_ref.at[pl.ds(step * QUERY_BLOCK, QUERY_BLOCK)]
            attend(step, weights_ref.at[step], total_ref.at[step], rows_out)
        return
    pl.when(pl.program_id(0) == 0)(norm)
    for step in range(steps):
        pl.when(pl.program_id(0) == step)(
            functools.partial(attend, step, weights_ref.at[0], total_ref.at[0], out_ref)
        )


def shards(signal, gate_rows, skip_gain, filter_taps, queries, key_rows):
    block, local_width = signal.shape
    heads_loc = filter_taps.shape[1]
    head_dim = local_width // heads_loc
    seq_count = lax.axis_size("seq")
    chan_count = lax.axis_size("chan")
    everyone = seq_count * chan_count
    length = block * seq_count
    sets = seq_count // heads_loc
    rows = block // sets
    channels = local_width // seq_count
    query_len = length // sets
    steps = query_len // QUERY_BLOCK
    gridded = length > 4096
    shape = jax.ShapeDtypeStruct

    def set_neighbour(array, offset):
        pairs = []
        for head in range(heads_loc):
            for part in range(sets):
                pairs.append((head * sets + (part + offset) % sets, head * sets + part))
        return lax.ppermute(array, "seq", pairs)

    split = call(
        split_kernel, shape((seq_count, 2, channels, block), BF16), moved=4 * signal.size * 2
    )(signal, gate_rows)
    split_got = lax.all_to_all(split, "seq", 0, 0, tiled=True)

    pack = call(
        functools.partial(pack_kernel, sets),
        shape((seq_count, 2, rows, head_dim), BF16),
        moved=4 * signal.size * 2,
    )(queries, key_rows)
    pack_got = lax.all_to_all(pack, "seq", 0, 0, tiled=True)

    matrix = call(
        functools.partial(toeplitz_kernel, sets),
        shape((block, length), BF16),
        moved=block * length * 2,
        flops=block * length * 8,
    )(filter_taps.T)
    skip = lax.dynamic_slice_in_dim(skip_gain, lax.axis_index("seq") * channels, channels)
    mixed, squares = call(
        conv_kernel,
        (
            shape((seq_count, channels, block), BF16),
            shape((everyone, seq_count, block), BF16),
        ),
        moved=split.size * 6,
        flops=length * length * channels,
        scratch_shapes=[pltpu.VMEM((seq_count * channels, block), F32)],
    )(split_got, matrix, skip[:, None])

    squares_got = lax.all_to_all(squares, ("seq", "chan"), 0, 0, tiled=True)
    mixed_others = [set_neighbour(mixed, offset) for offset in range(1, sets)]
    mixed_home = lax.all_to_all(mixed, "seq", 0, 0, tiled=True)

    key_others = [set_neighbour(pack_got[:, 1], offset) for offset in range(1, sets)]
    weights_shape = (steps, length, QUERY_BLOCK)
    total_shape = (steps, 8, QUERY_BLOCK)
    one = lambda dims: pl.BlockSpec((1,) + dims[1:], lambda step: (step, 0, 0))
    whole = pl.BlockSpec(memory_space=pltpu.VMEM)
    grid = dict(grid=(steps,), out_specs=(one(weights_shape), one(total_shape)))
    grid["in_specs"] = [whole] * sets
    weights, totals = call(
        functools.partial(weights_kernel, sets, gridded),
        (shape(weights_shape, BF16), shape(total_shape, F32)),
        moved=steps * length * QUERY_BLOCK * 2,
        flops=query_len * length * head_dim,
        exps=query_len * length // 2,
        scratch_shapes=[
            pltpu.VMEM((seq_count, sets, rows, head_dim), BF16),
            pltpu.VMEM((query_len, head_dim), BF16),
            pltpu.VMEM((length, QUERY_BLOCK), F32),
        ],
        **(grid if gridded else {}),
    )(pack_got, *key_others)

    grid = dict(grid=(steps,), out_specs=pl.BlockSpec((QUERY_BLOCK, head_dim), lambda step: (step, 0)))
    grid["in_specs"] = [whole, one(weights_shape), one(total_shape)] + [whole] * sets
    attended = call(
        functools.partial(output_kernel, sets, local_width * chan_count, gridded),
        shape((query_len, head_dim), BF16),
        moved=steps * length * QUERY_BLOCK * 2,
        flops=query_len * length * head_dim,
        scratch_shapes=[
            pltpu.VMEM((sets, channels, length), F32),
            pltpu.VMEM((head_dim, length), BF16),
        ],
        **(grid if gridded else {}),
    )(squares_got, weights, totals, mixed, *mixed_others)

    conv_mixed = call(unsplit_kernel, shape((block, local_width), BF16), moved=signal.size * 4)(
        mixed_home
    )
    return (conv_mixed, attended[None])


def solution(mesh):
    in_specs = (
        P("seq", "chan"),
        P("seq", "chan"),
        P("chan"),
        P(None, "chan"),
        P("seq", "chan"),
        P("seq", "chan"),
    )
    out_specs = (P("seq", "chan"), P(("chan", "seq"), None, None))
    return jax.shard_map(shards, mesh=mesh, in_specs=in_specs, out_specs=out_specs, check_vma=False)
```

```python
import functools
import math

import jax
import jax.numpy as jnp
from jax import lax
from jax.experimental import pallas as pl
from jax.experimental.pallas import tpu as pltpu
from jax.sharding import PartitionSpec as P

BF16, F32 = jnp.bfloat16, jnp.float32
QUERY_BLOCK = 256
KEY_CHUNK = 512
NT = (((1,), (1,)), ((), ()))


def call(kernel, out_shape, flops=0, exps=0, moved=0, vmem=8, **options):
    return pl.pallas_call(
        kernel,
        out_shape=out_shape,
        compiler_params=pltpu.CompilerParams(vmem_limit_bytes=vmem * 1024 * 1024),
        cost_estimate=pl.CostEstimate(flops=flops, bytes_accessed=moved, transcendentals=exps),
        **options,
    )


def merge_rows(blocks):
    count, rows, columns = blocks.shape
    if blocks.dtype == BF16 and rows % 16:
        return blocks.astype(F32).reshape(count * rows, columns).astype(BF16)
    return blocks.reshape(count * rows, columns)


def loop(count, body, carry):
    if count <= 8:
        for index in range(count):
            carry = body(index, carry)
        return carry
    return lax.fori_loop(0, count, body, carry)


def pack_kernel(sets, *refs):
    sources, (sent_ref, held_ref, semaphores) = refs[:4], refs[4:]
    count, _, rows, positions = sent_ref.shape
    head_dim = positions // 2
    copies = [
        pltpu.make_async_copy(source, held_ref.at[slot], semaphores.at[slot])
        for slot, source in enumerate(sources)
    ]
    for copy in copies:
        copy.start()
    for slot in (0, 1):
        copies[slot].wait()
        turned = held_ref[slot].astype(F32).T
        sent_ref[:, slot] = turned.reshape(count, rows, positions).astype(BF16)
    for slot in (2, 3):
        copies[slot].wait()
        for device in range(count):
            head, part = divmod(device, sets)
            first = part * 2 * rows
            lanes = slice(head * head_dim, (head + 1) * head_dim)
            sent_ref[device, slot] = side_by_side(held_ref[slot, first : first + 2 * rows, lanes])


def side_by_side(piece):
    rows = piece.shape[0] // 2
    if rows % 16:
        return side_by_side32(piece.astype(F32)).astype(BF16)
    return side_by_side32(piece)


def side_by_side32(piece):
    rows = piece.shape[0] // 2
    return jnp.concatenate([piece[:rows], piece[rows:]], axis=1)


def one_below_other(wide):
    columns = wide.shape[2] // 2
    if wide.shape[1] % 16:
        return one_below_other(wide.astype(F32)).astype(BF16) if wide.dtype == BF16 else (
            jnp.concatenate([wide[:, :, :columns], wide[:, :, columns:]], axis=1)
        )
    return jnp.concatenate([wide[:, :, :columns], wide[:, :, columns:]], axis=1)


def unpack_kernel(got_ref, out_ref):
    count = got_ref.shape[0]
    rows = out_ref.shape[1] // count
    whole = got_ref[:, :rows].astype(F32).reshape(count * rows, got_ref.shape[2])
    out_ref[...] = whole.T.astype(BF16)


def toeplitz_kernel(head_count_per, taps_ref, matrix_ref):
    block, length = matrix_ref.shape
    head = lax.axis_index("seq") // head_count_per
    taps = taps_ref[...].astype(F32)
    mine = lax.broadcasted_iota(jnp.int32, taps.shape, 0) == head
    row = jnp.sum(jnp.where(mine, taps, 0.0), axis=0, keepdims=True)
    rolled = pltpu.roll(jnp.broadcast_to(row, (block, length)), 0, 1, stride=1, stride_axis=0)
    source = lax.broadcasted_iota(jnp.int32, (block, block), 0)
    target = lax.broadcasted_iota(jnp.int32, (block, block), 1)
    matrix_ref[:, :block] = jnp.where(target >= source, rolled[:, :block], 0.0).astype(BF16)
    matrix_ref[:, block:] = rolled[:, block:].astype(BF16)


def conv_kernel(got_ref, matrix_ref, skip_ref, mixed_ref, back_ref, key_ref, total_ref):
    count, _, rows, block = got_ref.shape
    inputs = merge_rows(got_ref[:, 0])
    for lag in range(count):
        product = jnp.dot(
            inputs[: (count - lag) * rows],
            matrix_ref[:, lag * block : (lag + 1) * block],
            preferred_element_type=F32,
        )
        if lag == 0:
            total_ref[...] = product
        else:
            total_ref[lag * rows :] += product
    skip = skip_ref[...]
    sums = []
    for index in range(count):
        conv = total_ref[index * rows : (index + 1) * rows]
        direct = skip * got_ref[index, 0].astype(F32)
        mixed = (got_ref[index, 1].astype(F32) * (conv + direct)).astype(BF16)
        mixed_ref[index] = mixed
        back_ref[index, :rows] = mixed
        widened = mixed.astype(F32)
        sums.append(jnp.sum(widened * widened, axis=0, keepdims=True))
    squares = jnp.concatenate(sums, axis=0)
    high = squares.astype(BF16).astype(F32)
    both = jnp.concatenate([high, squares - high], axis=0).astype(BF16)
    for index in range(count):
        back_ref[index, rows:] = both
    key_ref[...] = one_below_other(got_ref[:, 3])


def weights_block(step, last, key_ref, query, sets, rows, scores_ref, weights_ref, total_ref):
    wide = query.shape[0]
    seq_block = sets * rows
    reach = wide // rows * seq_block
    chunk = min(KEY_CHUNK, reach)
    chunks = (step + 1) * reach // chunk
    head_dim = query.shape[1]
    factor = math.log2(math.e) / math.sqrt(head_dim)
    mine = lax.rem(lax.axis_index("seq"), sets)
    lane = step * wide + lax.broadcasted_iota(jnp.int32, (1, wide), 1)
    query_pos = lane // rows * seq_block + mine * rows + lax.rem(lane, rows)

    def score(index, peak):
        first = index * chunk
        part = key_ref[pl.ds(first, chunk), :]
        raw = lax.dot_general(part, query, NT, preferred_element_type=F32)
        if not isinstance(index, int) or first + chunk - 1 > step * reach:
            key_pos = first + lax.broadcasted_iota(jnp.int32, (chunk, 1), 0)
            raw = jnp.where(key_pos <= query_pos, raw, -jnp.inf)
        scores_ref[pl.ds(first, chunk), :] = raw
        return jnp.maximum(peak, jnp.max(raw, axis=0, keepdims=True))

    peak = loop(chunks, score, jnp.full((1, wide), -jnp.inf, F32))

    def weigh(index, total):
        first = index * chunk
        weights = jnp.exp2((scores_ref[pl.ds(first, chunk), :] - peak) * factor)
        weights_ref[pl.ds(first, chunk), :] = weights.astype(BF16)
        return total + jnp.sum(weights, axis=0, keepdims=True)

    total = loop(chunks, weigh, jnp.zeros((1, wide), F32))
    total_ref[...] = jnp.broadcast_to(total, total_ref.shape)


def weights_kernel(sets, gridded, got_ref, *refs):
    parts, (key_ref, query_ref, scores_ref) = refs[:sets], refs[-3:]
    total_ref, weights_refs = refs[sets], refs[sets + 1 : -3]
    count, _, rows, head_dim = key_ref.shape
    mine = lax.rem(lax.axis_index("seq"), sets)

    def assemble():
        query_ref[...] = merge_rows(one_below_other(got_ref[:, 2]))
        for offset in range(sets):
            place = lax.rem(mine + offset, sets)
            key_ref[:, pl.ds(place, 1)] = parts[offset][...][:, None]

    steps = query_ref.shape[0] // QUERY_BLOCK
    keys = key_ref.reshape(count * sets * rows, head_dim)

    def block(step, weights, total):
        query = query_ref[step * QUERY_BLOCK : (step + 1) * QUERY_BLOCK]
        weights_block(step, steps - 1, keys, query, sets, rows, scores_ref, weights, total)

    if not gridded:
        assemble()
        for step in range(steps):
            block(step, weights_refs[step], total_ref.at[step])
        return
    pl.when(pl.program_id(0) == 0)(assemble)
    for step in range(steps):
        pl.when(pl.program_id(0) == step)(
            functools.partial(block, step, weights_refs[0].at[0], total_ref.at[0])
        )


def output_kernel(sets, steps, width, gridded, *refs):
    squares_refs, refs = refs[: -4 - sets - (1 if gridded else steps)], refs[-4 - sets - (1 if gridded else steps) :]
    parts, total_ref, weights_refs = refs[:sets], refs[sets], refs[sets + 1 : -3]
    out_ref, wide_ref, values_ref = refs[-3:]
    count, rows, block = parts[0].shape
    mine = lax.rem(lax.axis_index("seq"), sets)
    reach = count * block // steps

    def norm():
        squares = sum(ref[...] for ref in squares_refs[1:]) + squares_refs[0][...]
        inv_scale = lax.rsqrt(squares / width + 1e-06)
        for offset in range(sets):
            place = lax.rem(mine + offset, sets)
            for index in range(count):
                part = parts[offset][index].astype(F32) * inv_scale[index : index + 1]
                wide_ref[place, :, index * block : (index + 1) * block] = part
        for index in range(count):
            span = slice(index * block, (index + 1) * block)
            values_ref[:, span] = merge_rows(wide_ref[:, :, span]).astype(BF16)

    def attend(step, weights, total, out):
        keys = (step + 1) * reach
        summed = jnp.dot(values_ref[:, :keys], weights[:keys], preferred_element_type=F32)
        out[...] = (summed / total[:1]).T.astype(BF16)

    if not gridded:
        norm()
        for step in range(steps):
            rows_out = out_ref.at[pl.ds(step * QUERY_BLOCK, QUERY_BLOCK)]
            attend(step, weights_refs[step], total_ref.at[step], rows_out)
        return
    pl.when(pl.program_id(0) == 0)(norm)
    for step in range(steps):
        pl.when(pl.program_id(0) == step)(
            functools.partial(attend, step, weights_refs[0].at[0], total_ref.at[0], out_ref)
        )


def shards(signal, gate_rows, skip_gain, filter_taps, queries, key_rows):
    block, local_width = signal.shape
    heads_loc = filter_taps.shape[1]
    head_dim = local_width // heads_loc
    seq_count = lax.axis_size("seq")
    chan_count = lax.axis_size("chan")
    everyone = seq_count * chan_count
    length = block * seq_count
    sets = seq_count // heads_loc
    rows = block // sets
    channels = local_width // seq_count
    query_len = length // sets
    steps = query_len // QUERY_BLOCK
    gridded = length > 4096
    shape = jax.ShapeDtypeStruct

    def set_neighbour(array, offset):
        pairs = []
        for head in range(heads_loc):
            for part in range(sets):
                pairs.append((head * sets + (part + offset) % sets, head * sets + part))
        return lax.ppermute(array, "seq", pairs)

    packed = call(
        functools.partial(pack_kernel, sets),
        shape((seq_count, 4, channels, block), BF16),
        moved=16 * signal.size,
        in_specs=[pl.BlockSpec(memory_space=pl.ANY)] * 4,
        vmem=56,
        scratch_shapes=[
            pltpu.VMEM((4,) + signal.shape, BF16),
            pltpu.SemaphoreType.DMA((4,)),
        ],
    )(signal, gate_rows, queries, key_rows)
    got = lax.all_to_all(packed, "seq", 0, 0, tiled=True)

    matrix = call(
        functools.partial(toeplitz_kernel, sets),
        shape((block, length), BF16),
        moved=block * length * 2,
        flops=block * length * 8,
        vmem=8 if not gridded else 56,
    )(filter_taps.T)
    skip = lax.dynamic_slice_in_dim(skip_gain, lax.axis_index("seq") * channels, channels)

    mixed, back, own_keys = call(
        conv_kernel,
        [
            shape((seq_count, channels, block), BF16),
            shape((seq_count, channels + 2 * seq_count, block), BF16),
            shape((seq_count, rows, head_dim), BF16),
        ],
        moved=signal.size * 10,
        flops=length * length * channels,
        vmem=8 if not gridded else 56,
        scratch_shapes=[pltpu.VMEM((seq_count * channels, block), F32)],
    )(got, matrix, skip[:, None])

    home = lax.all_to_all(back, "seq", 0, 0, tiled=True)
    key_parts = [own_keys] + [set_neighbour(own_keys, offset) for offset in range(1, sets)]
    mixed_parts = [mixed] + [set_neighbour(mixed, offset) for offset in range(1, sets)]
    squares = home[:, channels:].astype(F32).reshape(2 * seq_count, seq_count, block)
    squares = jnp.sum(squares, axis=0)
    all_squares = [squares]
    for offset in range(1, chan_count):
        pairs = [(source, (source + offset) % chan_count) for source in range(chan_count)]
        all_squares.append(lax.ppermute(squares, "chan", pairs))

    total_shape = (steps, 8, QUERY_BLOCK)
    one = lambda dims: pl.BlockSpec((1,) + dims[1:], lambda step: (step, 0, 0))
    whole = pl.BlockSpec(memory_space=pltpu.VMEM)
    if gridded:
        weights_shapes = [(steps, length, QUERY_BLOCK)]
        vmem = 56
        weights_specs = [one(total_shape), one(weights_shapes[0])]
        weights_grid = dict(grid=(steps,), in_specs=[whole] * (sets + 1), out_specs=weights_specs)
        output_grid = dict(
            grid=(steps,),
            in_specs=[whole] * (chan_count + sets) + weights_specs,
            out_specs=pl.BlockSpec((QUERY_BLOCK, head_dim), lambda step: (step, 0)),
        )
    else:
        weights_shapes = [(length * step // steps, QUERY_BLOCK) for step in range(1, steps + 1)]
        vmem = 12
        weights_grid = output_grid = {}
    totals, *weights = call(
        functools.partial(weights_kernel, sets, gridded),
        [shape(total_shape, F32)] + [shape(dims, BF16) for dims in weights_shapes],
        moved=2 * sum(math.prod(dims) for dims in weights_shapes),
        flops=query_len * length * head_dim,
        exps=query_len * length // 2,
        vmem=vmem,
        scratch_shapes=[
            pltpu.VMEM((seq_count, sets, rows, head_dim), BF16),
            pltpu.VMEM((query_len, head_dim), BF16),
            pltpu.VMEM((length, QUERY_BLOCK), F32),
        ],
        **weights_grid,
    )(got, *key_parts)

    attended = call(
        functools.partial(output_kernel, sets, steps, local_width * chan_count, gridded),
        shape((query_len, head_dim), BF16),
        moved=2 * sum(math.prod(dims) for dims in weights_shapes),
        flops=query_len * length * head_dim,
        vmem=vmem,
        scratch_shapes=[
            pltpu.VMEM((sets, channels, length), F32),
            pltpu.VMEM((head_dim, length), BF16),
        ],
        **output_grid,
    )(*all_squares, *mixed_parts, totals, *weights)

    conv_mixed = call(unpack_kernel, shape((block, local_width), BF16), moved=signal.size * 4)(home)
    return (conv_mixed, attended[None])


def solution(mesh):
    in_specs = (
        P("seq", "chan"),
        P("seq", "chan"),
        P("chan"),
        P(None, "chan"),
        P("seq", "chan"),
        P("seq", "chan"),
    )
    out_specs = (P("seq", "chan"), P(("chan", "seq"), None, None))
    return jax.shard_map(shards, mesh=mesh, in_specs=in_specs, out_specs=out_specs, check_vma=False)
```

```python
import functools
import math

import jax
import jax.numpy as jnp
from jax import lax
from jax.experimental import pallas as pl
from jax.experimental.pallas import tpu as pltpu
from jax.sharding import PartitionSpec as P

BF16, F32 = jnp.bfloat16, jnp.float32
QUERY_BLOCK = 256
KEY_CHUNK = 512
NT = (((1,), (1,)), ((), ()))


def call(kernel, out_shape, flops=0, exps=0, moved=0, vmem=8, **options):
    return pl.pallas_call(
        kernel,
        out_shape=out_shape,
        compiler_params=pltpu.CompilerParams(vmem_limit_bytes=vmem * 1024 * 1024),
        cost_estimate=pl.CostEstimate(flops=flops, bytes_accessed=moved, transcendentals=exps),
        **options,
    )


def merge_rows(blocks):
    count, rows, columns = blocks.shape
    if blocks.dtype == BF16 and rows % 16:
        return blocks.astype(F32).reshape(count * rows, columns).astype(BF16)
    return blocks.reshape(count * rows, columns)


def loop(count, body, carry):
    if count <= 8:
        for index in range(count):
            carry = body(index, carry)
        return carry
    return lax.fori_loop(0, count, body, carry)


def pack_kernel(signal_ref, gate_ref, sent_ref, held_ref, semaphores):
    count, _, rows, positions = sent_ref.shape
    copies = [
        pltpu.make_async_copy(source, held_ref.at[slot], semaphores.at[slot])
        for slot, source in enumerate((signal_ref, gate_ref))
    ]
    for copy in copies:
        copy.start()
    for slot, copy in enumerate(copies):
        copy.wait()
        turned = held_ref[slot].astype(F32).T
        sent_ref[:, slot] = turned.reshape(count, rows, positions).astype(BF16)


def heads_kernel(sets, query_ref, key_ref, *refs):
    pieces, semaphores = refs[:-1], refs[-1]
    head_dim = pieces[0].shape[2]
    mine = lax.axis_index("seq") // sets
    copies = []
    for offset, piece in enumerate(pieces):
        head = lax.rem(mine + offset, len(pieces))
        lanes = pl.ds(pl.multiple_of(head * head_dim, head_dim), head_dim)
        for slot, source in enumerate((query_ref, key_ref)):
            copies.append(
                pltpu.make_async_copy(
                    source.at[:, lanes], piece.at[slot], semaphores.at[offset, slot]
                )
            )
    for copy in copies:
        copy.start()
    for copy in copies:
        copy.wait()


def sets_kernel(sets, *refs):
    blocks = len(refs) - 2 - sets
    sources, keys_ref, queries_refs, semaphores = refs[:blocks], refs[blocks], refs[blocks + 1 : -1], refs[-1]
    rows = queries_refs[0].shape[1]
    mine = lax.rem(lax.axis_index("seq"), sets)
    copies = []
    for block, source in enumerate(sources):
        copies.append(
            pltpu.make_async_copy(source.at[1], keys_ref.at[block], semaphores.at[block, sets])
        )
        for offset, queries_ref in enumerate(queries_refs):
            part = lax.rem(mine + offset, sets)
            span = pl.ds(pl.multiple_of(part * rows, rows), rows)
            copies.append(
                pltpu.make_async_copy(
                    source.at[0, span], queries_ref.at[block], semaphores.at[block, offset]
                )
            )
    for copy in copies:
        copy.start()
    for copy in copies:
        copy.wait()


def arrange_kernel(sets, *refs):
    parts, (keys_ref, queries_ref, semaphores) = refs[: 2 * sets], refs[2 * sets :]
    heads = parts[0].shape[0]
    me = lax.axis_index("seq")
    copies = []
    for number, part in enumerate(parts):
        offset, arranged_ref = number % sets, (keys_ref, queries_ref)[number // sets]
        for index in range(heads):
            source = lax.rem(me // sets + heads - index, heads) * sets + lax.rem(me + offset, sets)
            copies.append(
                pltpu.make_async_copy(
                    part.at[index], arranged_ref.at[source], semaphores.at[number, index]
                )
            )
    for copy in copies:
        copy.start()
    for copy in copies:
        copy.wait()


def unpack_kernel(got_ref, out_ref):
    count = got_ref.shape[0]
    rows = out_ref.shape[1] // count
    whole = got_ref[:, :rows].astype(F32).reshape(count * rows, got_ref.shape[2])
    out_ref[...] = whole.T.astype(BF16)


def toeplitz_kernel(head_count_per, taps_ref, matrix_ref):
    block, length = matrix_ref.shape
    head = lax.axis_index("seq") // head_count_per
    taps = taps_ref[...].astype(F32)
    mine = lax.broadcasted_iota(jnp.int32, taps.shape, 0) == head
    row = jnp.sum(jnp.where(mine, taps, 0.0), axis=0, keepdims=True)
    rolled = pltpu.roll(jnp.broadcast_to(row, (block, length)), 0, 1, stride=1, stride_axis=0)
    source = lax.broadcasted_iota(jnp.int32, (block, block), 0)
    target = lax.broadcasted_iota(jnp.int32, (block, block), 1)
    matrix_ref[:, :block] = jnp.where(target >= source, rolled[:, :block], 0.0).astype(BF16)
    matrix_ref[:, block:] = rolled[:, block:].astype(BF16)


def conv_kernel(got_ref, matrix_ref, skip_ref, mixed_ref, back_ref, total_ref):
    count, _, rows, block = got_ref.shape
    inputs = merge_rows(got_ref[:, 0])
    for lag in range(count):
        product = jnp.dot(
            inputs[: (count - lag) * rows],
            matrix_ref[:, lag * block : (lag + 1) * block],
            preferred_element_type=F32,
        )
        if lag == 0:
            total_ref[...] = product
        else:
            total_ref[lag * rows :] += product
    skip = skip_ref[...]
    sums = []
    for index in range(count):
        conv = total_ref[index * rows : (index + 1) * rows]
        direct = skip * got_ref[index, 0].astype(F32)
        mixed = (got_ref[index, 1].astype(F32) * (conv + direct)).astype(BF16)
        mixed_ref[index] = mixed
        back_ref[index, :rows] = mixed
        widened = mixed.astype(F32)
        sums.append(jnp.sum(widened * widened, axis=0, keepdims=True))
    squares = jnp.concatenate(sums, axis=0)
    high = squares.astype(BF16).astype(F32)
    both = jnp.concatenate([high, squares - high], axis=0).astype(BF16)
    for index in range(count):
        back_ref[index, rows:] = both


def weights_block(step, last, key_ref, query, sets, rows, scores_ref, weights_ref, total_ref):
    wide = query.shape[0]
    seq_block = sets * rows
    reach = wide // rows * seq_block
    chunk = min(KEY_CHUNK, reach)
    chunks = (step + 1) * reach // chunk
    head_dim = query.shape[1]
    factor = math.log2(math.e) / math.sqrt(head_dim)
    mine = lax.rem(lax.axis_index("seq"), sets)
    lane = step * wide + lax.broadcasted_iota(jnp.int32, (1, wide), 1)
    query_pos = lane // rows * seq_block + mine * rows + lax.rem(lane, rows)

    def score(index, peak):
        first = index * chunk
        part = key_ref[pl.ds(first, chunk), :]
        raw = lax.dot_general(part, query, NT, preferred_element_type=F32)
        if not isinstance(index, int) or first + chunk - 1 > step * reach:
            key_pos = first + lax.broadcasted_iota(jnp.int32, (chunk, 1), 0)
            raw = jnp.where(key_pos <= query_pos, raw, -jnp.inf)
        scores_ref[pl.ds(first, chunk), :] = raw
        return jnp.maximum(peak, jnp.max(raw, axis=0, keepdims=True))

    peak = loop(chunks, score, jnp.full((1, wide), -jnp.inf, F32))

    def weigh(index, total):
        first = index * chunk
        weights = jnp.exp2((scores_ref[pl.ds(first, chunk), :] - peak) * factor)
        weights_ref[pl.ds(first, chunk), :] = weights.astype(BF16)
        return total + jnp.sum(weights, axis=0, keepdims=True)

    total = loop(chunks, weigh, jnp.zeros((1, wide), F32))
    total_ref[...] = jnp.broadcast_to(total, total_ref.shape)


def weights_kernel(gridded, key_ref, query_ref, total_ref, *refs):
    weights_refs, scores_ref = refs[:-1], refs[-1]
    count, positions, head_dim = key_ref.shape
    rows = query_ref.shape[1]
    sets = positions // rows
    steps = count * rows // QUERY_BLOCK
    keys = key_ref.reshape(count * positions, head_dim)

    def block(step, weights, total):
        each = QUERY_BLOCK // rows
        query = merge_rows(query_ref[step * each : (step + 1) * each])
        weights_block(step, steps - 1, keys, query, sets, rows, scores_ref, weights, total)

    if not gridded:
        for step in range(steps):
            block(step, weights_refs[step], total_ref.at[step])
        return
    for step in range(steps):
        pl.when(pl.program_id(0) == step)(
            functools.partial(block, step, weights_refs[0].at[0], total_ref.at[0])
        )


def output_kernel(sets, steps, width, gridded, *refs):
    squares_refs, refs = refs[: -4 - sets - (1 if gridded else steps)], refs[-4 - sets - (1 if gridded else steps) :]
    parts, total_ref, weights_refs = refs[:sets], refs[sets], refs[sets + 1 : -3]
    out_ref, wide_ref, values_ref = refs[-3:]
    count, rows, block = parts[0].shape
    mine = lax.rem(lax.axis_index("seq"), sets)
    reach = count * block // steps

    def norm():
        squares = sum(ref[...] for ref in squares_refs[1:]) + squares_refs[0][...]
        inv_scale = lax.rsqrt(squares / width + 1e-06)
        for offset in range(sets):
            place = lax.rem(mine + offset, sets)
            for index in range(count):
                part = parts[offset][index].astype(F32) * inv_scale[index : index + 1]
                wide_ref[place, :, index * block : (index + 1) * block] = part
        for index in range(count):
            span = slice(index * block, (index + 1) * block)
            values_ref[:, span] = merge_rows(wide_ref[:, :, span]).astype(BF16)

    def attend(step, weights, total, out):
        keys = (step + 1) * reach
        summed = jnp.dot(values_ref[:, :keys], weights[:keys], preferred_element_type=F32)
        out[...] = (summed / total[:1]).T.astype(BF16)

    if not gridded:
        norm()
        for step in range(steps):
            rows_out = out_ref.at[pl.ds(step * QUERY_BLOCK, QUERY_BLOCK)]
            attend(step, weights_refs[step], total_ref.at[step], rows_out)
        return
    pl.when(pl.program_id(0) == 0)(norm)
    for step in range(steps):
        pl.when(pl.program_id(0) == step)(
            functools.partial(attend, step, weights_refs[0].at[0], total_ref.at[0], out_ref)
        )


def shards(signal, gate_rows, skip_gain, filter_taps, queries, key_rows):
    block, local_width = signal.shape
    heads_loc = filter_taps.shape[1]
    head_dim = local_width // heads_loc
    seq_count = lax.axis_size("seq")
    chan_count = lax.axis_size("chan")
    everyone = seq_count * chan_count
    length = block * seq_count
    sets = seq_count // heads_loc
    rows = block // sets
    channels = local_width // seq_count
    query_len = length // sets
    steps = query_len // QUERY_BLOCK
    gridded = length > 4096
    shape = jax.ShapeDtypeStruct

    def from_set(array, offset):
        pairs = []
        for head in range(heads_loc):
            for part in range(sets):
                pairs.append((head * sets + (part + offset) % sets, head * sets + part))
        return lax.ppermute(array, "seq", pairs)

    def from_head(array, offset):
        pairs = [(source, (source + offset * sets) % seq_count) for source in range(seq_count)]
        return lax.ppermute(array, "seq", pairs)

    anywhere = pl.BlockSpec(memory_space=pl.ANY)
    packed = call(
        pack_kernel,
        shape((seq_count, 2, channels, block), BF16),
        moved=8 * signal.size,
        in_specs=[anywhere] * 2,
        vmem=56,
        scratch_shapes=[pltpu.VMEM((2,) + signal.shape, BF16), pltpu.SemaphoreType.DMA((2,))],
    )(signal, gate_rows)
    got = lax.all_to_all(packed, "seq", 0, 0, tiled=True)

    pieces = call(
        functools.partial(heads_kernel, sets),
        [shape((2, block, head_dim), BF16)] * heads_loc,
        moved=8 * signal.size,
        in_specs=[anywhere] * 2,
        out_specs=[anywhere] * heads_loc,
        scratch_shapes=[pltpu.SemaphoreType.DMA((heads_loc, 2))],
    )(queries, key_rows)
    pieces = [pieces[0]] + [from_head(pieces[k], k) for k in range(1, heads_loc)]
    own_keys, *set_queries = call(
        functools.partial(sets_kernel, sets),
        [shape((heads_loc, block, head_dim), BF16)] + [shape((heads_loc, rows, head_dim), BF16)] * sets,
        moved=8 * signal.size,
        flops=4 * 10**10,
        in_specs=[anywhere] * heads_loc,
        out_specs=[anywhere] * (sets + 1),
        scratch_shapes=[pltpu.SemaphoreType.DMA((heads_loc, sets + 1))],
    )(*pieces)
    key_parts = [own_keys] + [from_set(own_keys, k) for k in range(1, sets)]
    query_parts = [set_queries[0]] + [from_set(set_queries[-k], k) for k in range(1, sets)]

    matrix = call(
        functools.partial(toeplitz_kernel, sets),
        shape((block, length), BF16),
        moved=block * length * 2,
        flops=block * length * 8,
        vmem=8 if not gridded else 56,
    )(filter_taps.T)
    skip = lax.dynamic_slice_in_dim(skip_gain, lax.axis_index("seq") * channels, channels)

    whole = pl.BlockSpec(memory_space=pltpu.VMEM)
    mixed, back = call(
        conv_kernel,
        [
            shape((seq_count, channels, block), BF16),
            shape((seq_count, channels + 2 * seq_count, block), BF16),
        ],
        moved=signal.size * 10,
        flops=length * length * channels,
        vmem=8 if not gridded else 56,
        scratch_shapes=[pltpu.VMEM((seq_count * channels, block), F32)],
    )(got, matrix, skip[:, None])

    home = lax.all_to_all(back, "seq", 0, 0, tiled=True)
    mixed_parts = [mixed] + [from_set(mixed, offset) for offset in range(1, sets)]
    squares = home[:, channels:].astype(F32).reshape(2 * seq_count, seq_count, block)
    squares = jnp.sum(squares, axis=0)
    all_squares = [squares]
    for offset in range(1, chan_count):
        pairs = [(source, (source + offset) % chan_count) for source in range(chan_count)]
        all_squares.append(lax.ppermute(squares, "chan", pairs))

    total_shape = (steps, 8, QUERY_BLOCK)
    one = lambda dims: pl.BlockSpec((1,) + dims[1:], lambda step: (step, 0, 0))
    whole = pl.BlockSpec(memory_space=pltpu.VMEM)
    if gridded:
        weights_shapes = [(steps, length, QUERY_BLOCK)]
        vmem = 56
        weights_specs = [one(total_shape), one(weights_shapes[0])]
        weights_grid = dict(grid=(steps,), in_specs=[whole] * 2, out_specs=weights_specs)
        output_grid = dict(
            grid=(steps,),
            in_specs=[whole] * (chan_count + sets) + weights_specs,
            out_specs=pl.BlockSpec((QUERY_BLOCK, head_dim), lambda step: (step, 0)),
        )
    else:
        weights_shapes = [(length * step // steps, QUERY_BLOCK) for step in range(1, steps + 1)]
        vmem = 12
        weights_grid = output_grid = {}
    keys, arranged = call(
        functools.partial(arrange_kernel, sets),
        [shape((seq_count, block, head_dim), BF16), shape((seq_count, rows, head_dim), BF16)],
        moved=6 * length * head_dim,
        flops=4 * 10**10,
        in_specs=[anywhere] * (2 * sets),
        out_specs=[anywhere] * 2,
        scratch_shapes=[pltpu.SemaphoreType.DMA((2 * sets, heads_loc))],
    )(*key_parts, *query_parts)
    totals, *weights = call(
        functools.partial(weights_kernel, gridded),
        [shape(total_shape, F32)] + [shape(dims, BF16) for dims in weights_shapes],
        moved=2 * sum(math.prod(dims) for dims in weights_shapes),
        flops=query_len * length * head_dim,
        exps=query_len * length // 2,
        vmem=vmem,
        scratch_shapes=[
            pltpu.VMEM((length, QUERY_BLOCK), F32),
        ],
        **weights_grid,
    )(keys, arranged)

    attended = call(
        functools.partial(output_kernel, sets, steps, local_width * chan_count, gridded),
        shape((query_len, head_dim), BF16),
        moved=2 * sum(math.prod(dims) for dims in weights_shapes),
        flops=query_len * length * head_dim,
        vmem=vmem,
        scratch_shapes=[
            pltpu.VMEM((sets, channels, length), F32),
            pltpu.VMEM((head_dim, length), BF16),
        ],
        **output_grid,
    )(*all_squares, *mixed_parts, totals, *weights)

    conv_mixed = call(unpack_kernel, shape((block, local_width), BF16), moved=signal.size * 4)(home)
    return (conv_mixed, attended[None])


def solution(mesh):
    in_specs = (
        P("seq", "chan"),
        P("seq", "chan"),
        P("chan"),
        P(None, "chan"),
        P("seq", "chan"),
        P("seq", "chan"),
    )
    out_specs = (P("seq", "chan"), P(("chan", "seq"), None, None))
    return jax.shard_map(shards, mesh=mesh, in_specs=in_specs, out_specs=out_specs, check_vma=False)
```

```python
import functools
import math

import jax
import jax.numpy as jnp
from jax import lax
from jax.experimental import pallas as pl
from jax.experimental.pallas import tpu as pltpu
from jax.sharding import PartitionSpec as P

BF16, F32 = jnp.bfloat16, jnp.float32
QUERY_BLOCK = 256
KEY_CHUNK = 512
NT = (((1,), (1,)), ((), ()))


def call(kernel, out_shape, flops=0, exps=0, moved=0, vmem=8, **options):
    return pl.pallas_call(
        kernel,
        out_shape=out_shape,
        compiler_params=pltpu.CompilerParams(vmem_limit_bytes=vmem * 1024 * 1024),
        cost_estimate=pl.CostEstimate(flops=flops, bytes_accessed=moved, transcendentals=exps),
        **options,
    )


def merge_rows(blocks):
    count, rows, columns = blocks.shape
    if blocks.dtype == BF16 and rows % 16:
        return blocks.astype(F32).reshape(count * rows, columns).astype(BF16)
    return blocks.reshape(count * rows, columns)


def loop(count, body, carry):
    if count <= 8:
        for index in range(count):
            carry = body(index, carry)
        return carry
    return lax.fori_loop(0, count, body, carry)


def pack_kernel(sets, heads, signal_ref, gate_ref, query_ref, key_ref, *refs):
    sent_ref, key_refs, query_refs = refs[0], refs[1 : 1 + heads], refs[1 + heads : 1 + heads + sets]
    held_ref, split_ref, turned_ref, loads, stores = refs[1 + heads + sets :]
    _, count, rows, positions = turned_ref.shape
    head_dim = split_ref.shape[2]
    copies = [
        pltpu.make_async_copy(source, held_ref.at[slot], loads.at[slot])
        for slot, source in enumerate((key_ref, query_ref, signal_ref, gate_ref))
    ]
    for copy in copies:
        copy.start()
    me = lax.axis_index("seq")
    results = []

    def store(source, target):
        results.append(pltpu.make_async_copy(source, target, stores.at[len(results)]))
        results[-1].start()

    copies[0].wait()
    for offset, piece in enumerate(key_refs):
        head = lax.rem(me // sets + offset, heads)
        lanes = pl.ds(pl.multiple_of(head * head_dim, head_dim), head_dim)
        split_ref[offset] = held_ref[0, :, lanes]
        store(split_ref.at[offset], piece)
    copies[1].wait()
    for offset, piece in enumerate(query_refs):
        size = positions // sets
        first = lax.rem(me + offset, sets) * size
        store(held_ref.at[1, pl.ds(pl.multiple_of(first, size), size)], piece)
    for slot in (0, 1):
        copies[2 + slot].wait()
        turned = held_ref[2 + slot].astype(F32).T
        turned_ref[slot] = turned.reshape(count, rows, positions).astype(BF16)
        store(turned_ref.at[slot], sent_ref.at[:, slot])
    for result in results:
        result.wait()


def heads_kernel(sets, *refs):
    parts, pieces = refs[:sets], refs[sets:]
    head_dim = pieces[0].shape[2]
    mine = lax.axis_index("seq") // sets
    for offset, piece in enumerate(pieces):
        head = lax.rem(mine + offset, len(pieces))
        lanes = pl.ds(pl.multiple_of(head * head_dim, head_dim), head_dim)
        for index, part in enumerate(parts):
            piece[index] = part[:, lanes]


def join_kernel(*refs):
    pieces, (joined_ref, semaphores) = refs[:-2], refs[-2:]
    copies = [
        pltpu.make_async_copy(piece, joined_ref.at[index], semaphores.at[index])
        for index, piece in enumerate(pieces)
    ]
    for copy in copies:
        copy.start()
    for copy in copies:
        copy.wait()


def arrange_kernel(sets, *refs):
    key_parts, query_parts, (keys_ref, queries_ref, semaphores) = refs[:sets], refs[sets:-3], refs[-3:]
    heads = len(query_parts)
    me = lax.axis_index("seq")
    copies = []
    for index in range(heads):
        for offset in range(sets):
            source = lax.rem(me // sets + heads - index, heads) * sets + lax.rem(me + offset, sets)
            for slot, (part, target) in enumerate((
                (key_parts[offset].at[index], keys_ref.at[source]),
                (query_parts[index].at[offset], queries_ref.at[source]),
            )):
                semaphore = semaphores.at[slot, offset, index]
                copies.append(pltpu.make_async_copy(part, target, semaphore))
    for copy in copies:
        copy.start()
    for copy in copies:
        copy.wait()


def unpack_kernel(got_ref, out_ref):
    count = got_ref.shape[0]
    rows = out_ref.shape[1] // count
    whole = got_ref[:, :rows].astype(F32).reshape(count * rows, got_ref.shape[2])
    out_ref[...] = whole.T.astype(BF16)


def toeplitz_kernel(head_count_per, taps_ref, matrix_ref):
    block, length = matrix_ref.shape
    head = lax.axis_index("seq") // head_count_per
    taps = taps_ref[...].astype(F32)
    mine = lax.broadcasted_iota(jnp.int32, taps.shape, 0) == head
    row = jnp.sum(jnp.where(mine, taps, 0.0), axis=0, keepdims=True)
    rolled = pltpu.roll(jnp.broadcast_to(row, (block, length)), 0, 1, stride=1, stride_axis=0)
    source = lax.broadcasted_iota(jnp.int32, (block, block), 0)
    target = lax.broadcasted_iota(jnp.int32, (block, block), 1)
    matrix_ref[:, :block] = jnp.where(target >= source, rolled[:, :block], 0.0).astype(BF16)
    matrix_ref[:, block:] = rolled[:, block:].astype(BF16)


def conv_kernel(got_ref, matrix_ref, skip_ref, mixed_ref, back_ref, total_ref):
    count, _, rows, block = got_ref.shape
    inputs = merge_rows(got_ref[:, 0])
    for lag in range(count):
        product = jnp.dot(
            inputs[: (count - lag) * rows],
            matrix_ref[:, lag * block : (lag + 1) * block],
            preferred_element_type=F32,
        )
        if lag == 0:
            total_ref[...] = product
        else:
            total_ref[lag * rows :] += product
    skip = skip_ref[...]
    sums = []
    for index in range(count):
        conv = total_ref[index * rows : (index + 1) * rows]
        direct = skip * got_ref[index, 0].astype(F32)
        mixed = (got_ref[index, 1].astype(F32) * (conv + direct)).astype(BF16)
        mixed_ref[index] = mixed
        back_ref[index, :rows] = mixed
        widened = mixed.astype(F32)
        sums.append(jnp.sum(widened * widened, axis=0, keepdims=True))
    squares = jnp.concatenate(sums, axis=0)
    high = squares.astype(BF16).astype(F32)
    both = jnp.concatenate([high, squares - high], axis=0).astype(BF16)
    for index in range(count):
        back_ref[index, rows:] = both


def weights_block(step, last, key_ref, query, sets, rows, scores_ref, weights_ref, total_ref):
    wide = query.shape[0]
    seq_block = sets * rows
    reach = wide // rows * seq_block
    chunk = min(KEY_CHUNK, reach)
    chunks = (step + 1) * reach // chunk
    head_dim = query.shape[1]
    factor = math.log2(math.e) / math.sqrt(head_dim)
    mine = lax.rem(lax.axis_index("seq"), sets)
    lane = step * wide + lax.broadcasted_iota(jnp.int32, (1, wide), 1)
    query_pos = lane // rows * seq_block + mine * rows + lax.rem(lane, rows)

    def score(index, peak):
        first = index * chunk
        part = key_ref[pl.ds(first, chunk), :]
        raw = lax.dot_general(part, query, NT, preferred_element_type=F32)
        if not isinstance(index, int) or first + chunk - 1 > step * reach:
            key_pos = first + lax.broadcasted_iota(jnp.int32, (chunk, 1), 0)
            raw = jnp.where(key_pos <= query_pos, raw, -jnp.inf)
        scores_ref[pl.ds(first, chunk), :] = raw
        return jnp.maximum(peak, jnp.max(raw, axis=0, keepdims=True))

    peak = loop(chunks, score, jnp.full((1, wide), -jnp.inf, F32))

    def weigh(index, total):
        first = index * chunk
        weights = jnp.exp2((scores_ref[pl.ds(first, chunk), :] - peak) * factor)
        weights_ref[pl.ds(first, chunk), :] = weights.astype(BF16)
        return total + jnp.sum(weights, axis=0, keepdims=True)

    total = loop(chunks, weigh, jnp.zeros((1, wide), F32))
    total_ref[...] = jnp.broadcast_to(total, total_ref.shape)


def weights_kernel(gridded, key_ref, query_ref, total_ref, *refs):
    weights_refs, scores_ref = refs[:-1], refs[-1]
    count, positions, head_dim = key_ref.shape
    rows = query_ref.shape[1]
    sets = positions // rows
    steps = count * rows // QUERY_BLOCK
    keys = key_ref.reshape(count * positions, head_dim)

    def block(step, weights, total):
        each = QUERY_BLOCK // rows
        query = merge_rows(query_ref[step * each : (step + 1) * each])
        weights_block(step, steps - 1, keys, query, sets, rows, scores_ref, weights, total)

    if not gridded:
        for step in range(steps):
            block(step, weights_refs[step], total_ref.at[step])
        return
    for step in range(steps):
        pl.when(pl.program_id(0) == step)(
            functools.partial(block, step, weights_refs[0].at[0], total_ref.at[0])
        )


def output_kernel(sets, steps, width, gridded, *refs):
    squares_refs, refs = refs[: -4 - sets - (1 if gridded else steps)], refs[-4 - sets - (1 if gridded else steps) :]
    parts, total_ref, weights_refs = refs[:sets], refs[sets], refs[sets + 1 : -3]
    out_ref, wide_ref, values_ref = refs[-3:]
    count, rows, block = parts[0].shape
    mine = lax.rem(lax.axis_index("seq"), sets)
    reach = count * block // steps

    def norm():
        squares = sum(ref[...] for ref in squares_refs[1:]) + squares_refs[0][...]
        inv_scale = lax.rsqrt(squares / width + 1e-06)
        for offset in range(sets):
            place = lax.rem(mine + offset, sets)
            for index in range(count):
                part = parts[offset][index].astype(F32) * inv_scale[index : index + 1]
                wide_ref[place, :, index * block : (index + 1) * block] = part
        for index in range(count):
            span = slice(index * block, (index + 1) * block)
            values_ref[:, span] = merge_rows(wide_ref[:, :, span]).astype(BF16)

    def attend(step, weights, total, out):
        keys = (step + 1) * reach
        summed = jnp.dot(values_ref[:, :keys], weights[:keys], preferred_element_type=F32)
        out[...] = (summed / total[:1]).T.astype(BF16)

    if not gridded:
        norm()
        for step in range(steps):
            rows_out = out_ref.at[pl.ds(step * QUERY_BLOCK, QUERY_BLOCK)]
            attend(step, weights_refs[step], total_ref.at[step], rows_out)
        return
    pl.when(pl.program_id(0) == 0)(norm)
    for step in range(steps):
        pl.when(pl.program_id(0) == step)(
            functools.partial(attend, step, weights_refs[0].at[0], total_ref.at[0], out_ref)
        )


def shards(signal, gate_rows, skip_gain, filter_taps, queries, key_rows):
    block, local_width = signal.shape
    heads_loc = filter_taps.shape[1]
    head_dim = local_width // heads_loc
    seq_count = lax.axis_size("seq")
    chan_count = lax.axis_size("chan")
    everyone = seq_count * chan_count
    length = block * seq_count
    sets = seq_count // heads_loc
    rows = block // sets
    channels = local_width // seq_count
    query_len = length // sets
    steps = query_len // QUERY_BLOCK
    gridded = length > 4096
    shape = jax.ShapeDtypeStruct

    def from_set(array, offset):
        pairs = []
        for head in range(heads_loc):
            for part in range(sets):
                pairs.append((head * sets + (part + offset) % sets, head * sets + part))
        return lax.ppermute(array, "seq", pairs)

    def from_head(array, offset):
        pairs = [(source, (source + offset * sets) % seq_count) for source in range(seq_count)]
        return lax.ppermute(array, "seq", pairs)

    anywhere = pl.BlockSpec(memory_space=pl.ANY)
    packed, *pieces = call(
        functools.partial(pack_kernel, sets, heads_loc),
        [shape((seq_count, 2, channels, block), BF16)]
        + [shape((block, head_dim), BF16)] * heads_loc
        + [shape((rows, local_width), BF16)] * sets,
        moved=16 * signal.size,
        in_specs=[anywhere] * 4,
        out_specs=[anywhere] * (1 + heads_loc + sets),
        vmem=56,
        scratch_shapes=[
            pltpu.VMEM((4,) + signal.shape, BF16),
            pltpu.VMEM((heads_loc, block, head_dim), BF16),
            pltpu.VMEM((2, seq_count, channels, block), BF16),
            pltpu.SemaphoreType.DMA((4,)),
            pltpu.SemaphoreType.DMA((heads_loc + sets + 2,)),
        ],
    )(signal, gate_rows, queries, key_rows)
    got = lax.all_to_all(packed, "seq", 0, 0, tiled=True)
    key_pieces, set_queries = pieces[:heads_loc], pieces[heads_loc:]
    key_pieces = key_pieces[:1] + [from_head(key_pieces[k], k) for k in range(1, heads_loc)]
    own_keys = call(
        join_kernel,
        shape((heads_loc, block, head_dim), BF16),
        moved=4 * signal.size,
        flops=4 * 10**10,
        in_specs=[anywhere] * heads_loc,
        out_specs=anywhere,
        scratch_shapes=[pltpu.SemaphoreType.DMA((heads_loc,))],
    )(*key_pieces)
    key_parts = [own_keys] + [from_set(own_keys, k) for k in range(1, sets)]
    query_sets = set_queries[:1] + [from_set(set_queries[-k], k) for k in range(1, sets)]
    query_pieces = call(
        functools.partial(heads_kernel, sets),
        [shape((sets, rows, head_dim), BF16)] * heads_loc,
        moved=4 * signal.size,
        flops=0,
    )(*query_sets)
    query_parts = [query_pieces[0]] + [from_head(query_pieces[k], k) for k in range(1, heads_loc)]

    matrix = call(
        functools.partial(toeplitz_kernel, sets),
        shape((block, length), BF16),
        moved=block * length * 2,
        flops=block * length * 8,
        vmem=8 if not gridded else 56,
    )(filter_taps.T)
    skip = lax.dynamic_slice_in_dim(skip_gain, lax.axis_index("seq") * channels, channels)

    whole = pl.BlockSpec(memory_space=pltpu.VMEM)
    mixed, back = call(
        conv_kernel,
        [
            shape((seq_count, channels, block), BF16),
            shape((seq_count, channels + 2 * seq_count, block), BF16),
        ],
        moved=signal.size * 10,
        flops=length * length * channels,
        vmem=8 if not gridded else 56,
        scratch_shapes=[pltpu.VMEM((seq_count * channels, block), F32)],
    )(got, matrix, skip[:, None])

    home = lax.all_to_all(back, "seq", 0, 0, tiled=True)
    mixed_parts = [mixed] + [from_set(mixed, offset) for offset in range(1, sets)]
    squares = home[:, channels:].astype(F32).reshape(2 * seq_count, seq_count, block)
    squares = jnp.sum(squares, axis=0)
    all_squares = [squares]
    for offset in range(1, chan_count):
        pairs = [(source, (source + offset) % chan_count) for source in range(chan_count)]
        all_squares.append(lax.ppermute(squares, "chan", pairs))

    total_shape = (steps, 8, QUERY_BLOCK)
    one = lambda dims: pl.BlockSpec((1,) + dims[1:], lambda step: (step, 0, 0))
    whole = pl.BlockSpec(memory_space=pltpu.VMEM)
    if gridded:
        weights_shapes = [(steps, length, QUERY_BLOCK)]
        vmem = 56
        weights_specs = [one(total_shape), one(weights_shapes[0])]
        weights_grid = dict(grid=(steps,), in_specs=[whole] * 2, out_specs=weights_specs)
        output_grid = dict(
            grid=(steps,),
            in_specs=[whole] * (chan_count + sets) + weights_specs,
            out_specs=pl.BlockSpec((QUERY_BLOCK, head_dim), lambda step: (step, 0)),
        )
    else:
        weights_shapes = [(length * step // steps, QUERY_BLOCK) for step in range(1, steps + 1)]
        vmem = 12
        weights_grid = output_grid = {}
    keys, arranged = call(
        functools.partial(arrange_kernel, sets),
        [shape((seq_count, block, head_dim), BF16), shape((seq_count, rows, head_dim), BF16)],
        moved=6 * length * head_dim,
        flops=4 * 10**10,
        in_specs=[anywhere] * (sets + heads_loc),
        out_specs=[anywhere] * 2,
        scratch_shapes=[pltpu.SemaphoreType.DMA((2, sets, heads_loc))],
    )(*key_parts, *query_parts)
    totals, *weights = call(
        functools.partial(weights_kernel, gridded),
        [shape(total_shape, F32)] + [shape(dims, BF16) for dims in weights_shapes],
        moved=2 * sum(math.prod(dims) for dims in weights_shapes),
        flops=query_len * length * head_dim,
        exps=query_len * length // 2,
        vmem=vmem,
        scratch_shapes=[
            pltpu.VMEM((length, QUERY_BLOCK), F32),
        ],
        **weights_grid,
    )(keys, arranged)

    attended = call(
        functools.partial(output_kernel, sets, steps, local_width * chan_count, gridded),
        shape((query_len, head_dim), BF16),
        moved=2 * sum(math.prod(dims) for dims in weights_shapes),
        flops=query_len * length * head_dim,
        vmem=vmem,
        scratch_shapes=[
            pltpu.VMEM((sets, channels, length), F32),
            pltpu.VMEM((head_dim, length), BF16),
        ],
        **output_grid,
    )(*all_squares, *mixed_parts, totals, *weights)

    conv_mixed = call(unpack_kernel, shape((block, local_width), BF16), moved=signal.size * 4)(home)
    return (conv_mixed, attended[None])


def solution(mesh):
    in_specs = (
        P("seq", "chan"),
        P("seq", "chan"),
        P("chan"),
        P(None, "chan"),
        P("seq", "chan"),
        P("seq", "chan"),
    )
    out_specs = (P("seq", "chan"), P(("chan", "seq"), None, None))
    return jax.shard_map(shards, mesh=mesh, in_specs=in_specs, out_specs=out_specs, check_vma=False)
```

```python
import functools
import math

import jax
import jax.numpy as jnp
from jax import lax
from jax.experimental import pallas as pl
from jax.experimental.pallas import tpu as pltpu
from jax.sharding import PartitionSpec as P

BF16, F32 = jnp.bfloat16, jnp.float32
QUERY_BLOCK = 256
KEY_CHUNK = 512
NT = (((1,), (1,)), ((), ()))


def call(kernel, out_shape, flops=0, exps=0, moved=0, vmem=8, **options):
    return pl.pallas_call(
        kernel,
        out_shape=out_shape,
        compiler_params=pltpu.CompilerParams(vmem_limit_bytes=vmem * 1024 * 1024),
        cost_estimate=pl.CostEstimate(flops=flops, bytes_accessed=moved, transcendentals=exps),
        **options,
    )


def merge_rows(blocks):
    count, rows, columns = blocks.shape
    if blocks.dtype == BF16 and rows % 16:
        return blocks.astype(F32).reshape(count * rows, columns).astype(BF16)
    return blocks.reshape(count * rows, columns)


def loop(count, body, carry):
    if count <= 8:
        for index in range(count):
            carry = body(index, carry)
        return carry
    return lax.fori_loop(0, count, body, carry)


def pack_kernel(sets, heads, signal_ref, gate_ref, query_ref, key_ref, *refs):
    sent_ref, key_refs, query_refs = refs[0], refs[1 : 1 + heads], refs[1 + heads : 1 + heads + sets]
    held_ref, split_ref, turned_ref, loads, stores = refs[1 + heads + sets :]
    _, count, rows, positions = turned_ref.shape
    head_dim = split_ref.shape[2]
    copies = [
        pltpu.make_async_copy(source, held_ref.at[slot], loads.at[slot])
        for slot, source in enumerate((key_ref, query_ref, signal_ref, gate_ref))
    ]
    for copy in copies:
        copy.start()
    me = lax.axis_index("seq")
    results = []

    def store(source, target):
        results.append(pltpu.make_async_copy(source, target, stores.at[len(results)]))
        results[-1].start()

    copies[0].wait()
    for offset, piece in enumerate(key_refs):
        head = lax.rem(me // sets + offset, heads)
        lanes = pl.ds(pl.multiple_of(head * head_dim, head_dim), head_dim)
        split_ref[offset] = held_ref[0, :, lanes]
        store(split_ref.at[offset], piece)
    copies[1].wait()
    for offset, piece in enumerate(query_refs):
        size = positions // sets
        first = lax.rem(me + offset, sets) * size
        store(held_ref.at[1, pl.ds(pl.multiple_of(first, size), size)], piece)
    for slot in (0, 1):
        copies[2 + slot].wait()
        turned = held_ref[2 + slot].astype(F32).T
        turned_ref[slot] = turned.reshape(count, rows, positions).astype(BF16)
        store(turned_ref.at[slot], sent_ref.at[:, slot])
    for result in results:
        result.wait()


def heads_kernel(sets, *refs):
    parts, pieces = refs[:sets], refs[sets:]
    head_dim = pieces[0].shape[2]
    mine = lax.axis_index("seq") // sets
    for offset, piece in enumerate(pieces):
        head = lax.rem(mine + offset, len(pieces))
        lanes = pl.ds(pl.multiple_of(head * head_dim, head_dim), head_dim)
        for index, part in enumerate(parts):
            piece[index] = part[:, lanes]


def join_kernel(count, *refs):
    pieces, (joined_ref, semaphores) = refs[:count], refs[-2:]
    copies = [
        pltpu.make_async_copy(piece, joined_ref.at[index], semaphores.at[index])
        for index, piece in enumerate(pieces)
    ]
    for copy in copies:
        copy.start()
    for copy in copies:
        copy.wait()


def arrange_kernel(sets, *refs):
    key_parts, query_parts, (keys_ref, queries_ref, semaphores) = refs[:sets], refs[sets:-3], refs[-3:]
    heads = len(query_parts)
    me = lax.axis_index("seq")
    copies = []
    for index in range(heads):
        for offset in range(sets):
            source = lax.rem(me // sets + heads - index, heads) * sets + lax.rem(me + offset, sets)
            for slot, (part, target) in enumerate((
                (key_parts[offset].at[index], keys_ref.at[source]),
                (query_parts[index].at[offset], queries_ref.at[source]),
            )):
                semaphore = semaphores.at[slot, offset, index]
                copies.append(pltpu.make_async_copy(part, target, semaphore))
    for copy in copies:
        copy.start()
    for copy in copies:
        copy.wait()


def unpack_kernel(got_ref, out_ref):
    count = got_ref.shape[0]
    rows = out_ref.shape[1] // count
    whole = got_ref[:, :rows].astype(F32).reshape(count * rows, got_ref.shape[2])
    out_ref[...] = whole.T.astype(BF16)


def toeplitz_kernel(head_count_per, taps_ref, matrix_ref):
    block, length = matrix_ref.shape
    head = lax.axis_index("seq") // head_count_per
    taps = taps_ref[...].astype(F32)
    mine = lax.broadcasted_iota(jnp.int32, taps.shape, 0) == head
    row = jnp.sum(jnp.where(mine, taps, 0.0), axis=0, keepdims=True)
    rolled = pltpu.roll(jnp.broadcast_to(row, (block, length)), 0, 1, stride=1, stride_axis=0)
    source = lax.broadcasted_iota(jnp.int32, (block, block), 0)
    target = lax.broadcasted_iota(jnp.int32, (block, block), 1)
    matrix_ref[:, :block] = jnp.where(target >= source, rolled[:, :block], 0.0).astype(BF16)
    matrix_ref[:, block:] = rolled[:, block:].astype(BF16)


def conv_kernel(got_ref, matrix_ref, skip_ref, mixed_ref, back_ref, total_ref):
    count, _, rows, block = got_ref.shape
    inputs = merge_rows(got_ref[:, 0])
    before = jnp.concatenate([jnp.zeros((rows, block), BF16), inputs[: (count - 1) * rows]], axis=0)
    pairs = jnp.concatenate([inputs, before], axis=1)
    for lag in range(0, count, 2):
        spans = [slice((lag + more) * block, (lag + more + 1) * block) for more in (0, 1)]
        product = jnp.dot(
            pairs[: (count - lag) * rows],
            jnp.concatenate([matrix_ref[:, span] for span in spans], axis=0),
            preferred_element_type=F32,
        )
        if lag == 0:
            total_ref[...] = product
        else:
            total_ref[lag * rows :] += product
    skip = skip_ref[...]
    sums = []
    for index in range(count):
        conv = total_ref[index * rows : (index + 1) * rows]
        direct = skip * got_ref[index, 0].astype(F32)
        mixed = (got_ref[index, 1].astype(F32) * (conv + direct)).astype(BF16)
        mixed_ref[index] = mixed
        back_ref[index, :rows] = mixed
        widened = mixed.astype(F32)
        sums.append(jnp.sum(widened * widened, axis=0, keepdims=True))
    squares = jnp.concatenate(sums, axis=0)
    both = squares.astype(BF16)
    for index in range(count):
        back_ref[index, rows:] = both


def weights_block(step, last, key_ref, query, sets, rows, scores_ref, weights_ref, total_ref):
    wide = query.shape[0]
    seq_block = sets * rows
    reach = wide // rows * seq_block
    chunk = min(KEY_CHUNK, reach)
    chunks = (step + 1) * reach // chunk
    head_dim = query.shape[1]
    factor = math.log2(math.e) / math.sqrt(head_dim)
    mine = lax.rem(lax.axis_index("seq"), sets)
    lane = step * wide + lax.broadcasted_iota(jnp.int32, (1, wide), 1)
    query_pos = lane // rows * seq_block + mine * rows + lax.rem(lane, rows)

    def score(index, peak):
        first = index * chunk
        part = key_ref[pl.ds(first, chunk), :]
        raw = lax.dot_general(part, query, NT, preferred_element_type=F32)
        if not isinstance(index, int) or first + chunk - 1 > step * reach:
            key_pos = first + lax.broadcasted_iota(jnp.int32, (chunk, 1), 0)
            raw = jnp.where(key_pos <= query_pos, raw, -jnp.inf)
        scores_ref[pl.ds(first, chunk), :] = raw
        return jnp.maximum(peak, jnp.max(raw, axis=0, keepdims=True))

    peak = loop(chunks, score, jnp.full((1, wide), -jnp.inf, F32))

    def weigh(index, total):
        first = index * chunk
        weights = jnp.exp2((scores_ref[pl.ds(first, chunk), :] - peak) * factor)
        weights_ref[pl.ds(first, chunk), :] = weights.astype(BF16)
        return total + jnp.sum(weights, axis=0, keepdims=True)

    total = loop(chunks, weigh, jnp.zeros((1, wide), F32))
    total_ref[...] = jnp.broadcast_to(1.0 / total, total_ref.shape)


def weights_kernel(gridded, key_ref, query_ref, total_ref, *refs):
    weights_refs, scores_ref = refs[:-1], refs[-1]
    count, positions, head_dim = key_ref.shape
    rows = query_ref.shape[1]
    sets = positions // rows
    steps = count * rows // QUERY_BLOCK
    keys = key_ref.reshape(count * positions, head_dim)

    def block(step, weights, total):
        each = QUERY_BLOCK // rows
        query = merge_rows(query_ref[step * each : (step + 1) * each])
        weights_block(step, steps - 1, keys, query, sets, rows, scores_ref, weights, total)

    if not gridded:
        for step in range(steps):
            block(step, weights_refs[step], total_ref.at[step])
        return
    for step in range(steps):
        pl.when(pl.program_id(0) == step)(
            functools.partial(block, step, weights_refs[0].at[0], total_ref.at[0])
        )


def output_kernel(sets, steps, width, gridded, *refs):
    own = 4 if gridded else 6
    first = len(refs) - own - sets - (1 if gridded else steps)
    squares_refs, parts, refs = refs[:first], refs[first : first + sets], refs[first + sets :]
    total_ref, weights_refs, refs = refs[0], refs[1 : 1 - own], refs[1 - own :]
    out_ref, wide_ref, values_ref = refs[:3]
    count, rows, block = parts[0].shape
    mine = lax.rem(lax.axis_index("seq"), sets)
    reach = count * block // steps

    def norm():
        squares = sum(ref[...] for ref in squares_refs[1:]) + squares_refs[0][...]
        inv_scale = lax.rsqrt(squares / width + 1e-06)
        for offset in range(sets):
            place = lax.rem(mine + offset, sets)
            for index in range(count):
                span = slice(index * block, (index + 1) * block)
                part = parts[offset][index].astype(F32) * inv_scale[index : index + 1]
                if rows % 16:
                    wide_ref[place, :, span] = part
                else:
                    lines = pl.ds(pl.multiple_of(place * rows, rows), rows)
                    values_ref[lines, span] = part.astype(BF16)
        if rows % 16:
            for index in range(count):
                span = slice(index * block, (index + 1) * block)
                values_ref[:, span] = merge_rows(wide_ref[:, :, span]).astype(BF16)

    def attend(step, weights, total):
        keys = (step + 1) * reach
        summed = jnp.dot(values_ref[:, :keys], weights[:keys], preferred_element_type=F32)
        return (summed * total[:1]).T.astype(BF16)

    if gridded:
        pl.when(pl.program_id(0) == 0)(norm)

        def block_of(step):
            out_ref[...] = attend(step, weights_refs[0].at[0], total_ref.at[0])

        for step in range(steps):
            pl.when(pl.program_id(0) == step)(functools.partial(block_of, step))
        return
    staged_ref, semaphores = refs[3:]
    norm()
    copies = []
    for step in reversed(range(steps)):
        staged_ref[step] = attend(step, weights_refs[step], total_ref.at[step])
        lines = out_ref.at[pl.ds(step * QUERY_BLOCK, QUERY_BLOCK)]
        copies.append(pltpu.make_async_copy(staged_ref.at[step], lines, semaphores.at[step]))
        copies[-1].start()
    for copy in copies:
        copy.wait()


def shards(signal, gate_rows, skip_gain, filter_taps, queries, key_rows):
    block, local_width = signal.shape
    heads_loc = filter_taps.shape[1]
    head_dim = local_width // heads_loc
    seq_count = lax.axis_size("seq")
    chan_count = lax.axis_size("chan")
    everyone = seq_count * chan_count
    length = block * seq_count
    sets = seq_count // heads_loc
    rows = block // sets
    channels = local_width // seq_count
    query_len = length // sets
    steps = query_len // QUERY_BLOCK
    gridded = length > 4096
    shape = jax.ShapeDtypeStruct

    def from_set(array, offset):
        pairs = []
        for head in range(heads_loc):
            for part in range(sets):
                pairs.append((head * sets + (part + offset) % sets, head * sets + part))
        return lax.ppermute(array, "seq", pairs)

    def from_head(array, offset):
        pairs = [(source, (source + offset * sets) % seq_count) for source in range(seq_count)]
        return lax.ppermute(array, "seq", pairs)

    anywhere = pl.BlockSpec(memory_space=pl.ANY)
    packed, *pieces = call(
        functools.partial(pack_kernel, sets, heads_loc),
        [shape((seq_count, 2, channels, block), BF16)]
        + [shape((block, head_dim), BF16)] * heads_loc
        + [shape((rows, local_width), BF16)] * sets,
        moved=16 * signal.size,
        in_specs=[anywhere] * 4,
        out_specs=[anywhere] * (1 + heads_loc + sets),
        vmem=56,
        scratch_shapes=[
            pltpu.VMEM((4,) + signal.shape, BF16),
            pltpu.VMEM((heads_loc, block, head_dim), BF16),
            pltpu.VMEM((2, seq_count, channels, block), BF16),
            pltpu.SemaphoreType.DMA((4,)),
            pltpu.SemaphoreType.DMA((heads_loc + sets + 2,)),
        ],
    )(signal, gate_rows, queries, key_rows)
    got = lax.all_to_all(packed, "seq", 0, 0, tiled=True)
    key_pieces, set_queries = pieces[:heads_loc], pieces[heads_loc:]
    key_pieces = key_pieces[:1] + [from_head(key_pieces[k], k) for k in range(1, heads_loc)]
    matrix = call(
        functools.partial(toeplitz_kernel, sets),
        shape((block, length), BF16),
        moved=block * length * 2,
        flops=block * length * 8,
        vmem=8 if not gridded else 56,
    )(filter_taps.T)
    skip = lax.dynamic_slice_in_dim(skip_gain, lax.axis_index("seq") * channels, channels)[:, None]

    whole = pl.BlockSpec(memory_space=pltpu.VMEM)
    own_keys = call(
        functools.partial(join_kernel, heads_loc),
        shape((heads_loc, block, head_dim), BF16),
        moved=4 * signal.size,
        flops=4 * 10**10,
        in_specs=[anywhere] * (heads_loc + 1),
        out_specs=anywhere,
        scratch_shapes=[pltpu.SemaphoreType.DMA((heads_loc,))],
    )(*key_pieces, matrix)
    key_parts = [own_keys] + [from_set(own_keys, k) for k in range(1, sets)]
    query_sets = set_queries[:1] + [from_set(set_queries[-k], k) for k in range(1, sets)]
    query_pieces = call(
        functools.partial(heads_kernel, sets),
        [shape((sets, rows, head_dim), BF16)] * heads_loc,
        moved=4 * signal.size,
        flops=0,
    )(*query_sets)
    query_parts = [query_pieces[0]] + [from_head(query_pieces[k], k) for k in range(1, heads_loc)]

    mixed, back = call(
        conv_kernel,
        [
            shape((seq_count, channels, block), BF16),
            shape((seq_count, channels + seq_count, block), BF16),
        ],
        moved=signal.size * 10,
        flops=length * length * channels,
        vmem=8 if not gridded else 56,
        scratch_shapes=[pltpu.VMEM((seq_count * channels, block), F32)],
    )(got, matrix, skip)

    home = lax.all_to_all(back, "seq", 0, 0, tiled=True)
    mixed_parts = [mixed] + [from_set(mixed, offset) for offset in range(1, sets)]
    squares = home[:, channels:].astype(F32).reshape(seq_count, seq_count, block)
    squares = jnp.sum(squares, axis=0)
    all_squares = [squares]
    for offset in range(1, chan_count):
        pairs = [(source, (source + offset) % chan_count) for source in range(chan_count)]
        all_squares.append(lax.ppermute(squares, "chan", pairs))

    total_shape = (steps, 8, QUERY_BLOCK)
    one = lambda dims: pl.BlockSpec((1,) + dims[1:], lambda step: (step, 0, 0))
    whole = pl.BlockSpec(memory_space=pltpu.VMEM)
    if gridded:
        weights_shapes = [(steps, length, QUERY_BLOCK)]
        vmem = 56
        weights_specs = [one(total_shape), one(weights_shapes[0])]
        weights_grid = dict(grid=(steps,), in_specs=[whole] * 2, out_specs=weights_specs)
        output_grid = dict(
            grid=(steps,),
            in_specs=[whole] * (chan_count + sets) + weights_specs,
            out_specs=pl.BlockSpec((QUERY_BLOCK, head_dim), lambda step: (step, 0)),
        )
    else:
        weights_shapes = [(length * step // steps, QUERY_BLOCK) for step in range(1, steps + 1)]
        vmem = 12
        weights_grid = {}
        output_grid = dict(
            in_specs=[whole] * (chan_count + sets + 1 + steps),
            out_specs=anywhere,
        )
        output_scratch = [
            pltpu.VMEM((steps, QUERY_BLOCK, head_dim), BF16),
            pltpu.SemaphoreType.DMA((steps,)),
        ]
    keys, arranged = call(
        functools.partial(arrange_kernel, sets),
        [shape((seq_count, block, head_dim), BF16), shape((seq_count, rows, head_dim), BF16)],
        moved=6 * length * head_dim,
        flops=4 * 10**10,
        in_specs=[anywhere] * (sets + heads_loc),
        out_specs=[anywhere] * 2,
        scratch_shapes=[pltpu.SemaphoreType.DMA((2, sets, heads_loc))],
    )(*key_parts, *query_parts)
    totals, *weights = call(
        functools.partial(weights_kernel, gridded),
        [shape(total_shape, F32)] + [shape(dims, BF16) for dims in weights_shapes],
        moved=2 * sum(math.prod(dims) for dims in weights_shapes),
        flops=query_len * length * head_dim,
        exps=query_len * length // 2,
        vmem=vmem,
        scratch_shapes=[
            pltpu.VMEM((length, QUERY_BLOCK), F32),
        ],
        **weights_grid,
    )(keys, arranged)

    attended = call(
        functools.partial(output_kernel, sets, steps, local_width * chan_count, gridded),
        shape((query_len, head_dim), BF16),
        moved=2 * sum(math.prod(dims) for dims in weights_shapes),
        flops=query_len * length * head_dim,
        vmem=vmem,
        scratch_shapes=[
            pltpu.VMEM((sets, channels, length if channels % 16 else block), F32),
            pltpu.VMEM((head_dim, length), BF16),
        ]
        + ([] if gridded else output_scratch),
        **output_grid,
    )(*all_squares, *mixed_parts, totals, *weights)

    conv_mixed = call(unpack_kernel, shape((block, local_width), BF16), moved=signal.size * 4)(home)
    return (conv_mixed, attended[None])


def solution(mesh):
    in_specs = (
        P("seq", "chan"),
        P("seq", "chan"),
        P("chan"),
        P(None, "chan"),
        P("seq", "chan"),
        P("seq", "chan"),
    )
    out_specs = (P("seq", "chan"), P(("chan", "seq"), None, None))
    return jax.shard_map(shards, mesh=mesh, in_specs=in_specs, out_specs=out_specs, check_vma=False)
```

```python
import functools
import math

import jax
import jax.numpy as jnp
from jax import lax
from jax.experimental import pallas as pl
from jax.experimental.pallas import tpu as pltpu
from jax.sharding import PartitionSpec as P

BF16, F32 = jnp.bfloat16, jnp.float32
QUERY_BLOCK = 256
KEY_CHUNK = 512
NT = (((1,), (1,)), ((), ()))


def call(kernel, out_shape, flops=0, exps=0, moved=0, vmem=8, **options):
    return pl.pallas_call(
        kernel,
        out_shape=out_shape,
        compiler_params=pltpu.CompilerParams(vmem_limit_bytes=vmem * 1024 * 1024),
        cost_estimate=pl.CostEstimate(flops=flops, bytes_accessed=moved, transcendentals=exps),
        **options,
    )


def merge_rows(blocks):
    count, rows, columns = blocks.shape
    if blocks.dtype == BF16 and rows % 16:
        return blocks.astype(F32).reshape(count * rows, columns).astype(BF16)
    return blocks.reshape(count * rows, columns)


def loop(count, body, carry):
    if count <= 8:
        for index in range(count):
            carry = body(index, carry)
        return carry
    return lax.fori_loop(0, count, body, carry)


def pack_kernel(sets, heads, signal_ref, gate_ref, query_ref, key_ref, *refs):
    sent_ref, key_refs, query_refs = refs[0], refs[1 : 1 + heads], refs[1 + heads : 1 + heads + sets]
    held_ref, split_ref, turned_ref, loads, stores = refs[1 + heads + sets :]
    _, count, rows, positions = turned_ref.shape
    head_dim = split_ref.shape[2]
    copies = [
        pltpu.make_async_copy(source, held_ref.at[slot], loads.at[slot])
        for slot, source in enumerate((key_ref, query_ref, signal_ref, gate_ref))
    ]
    for copy in copies:
        copy.start()
    me = lax.axis_index("seq")
    results = []

    def store(source, target):
        results.append(pltpu.make_async_copy(source, target, stores.at[len(results)]))
        results[-1].start()

    copies[0].wait()
    for offset, piece in enumerate(key_refs):
        head = lax.rem(me // sets + offset, heads)
        lanes = pl.ds(pl.multiple_of(head * head_dim, head_dim), head_dim)
        split_ref[offset] = held_ref[0, :, lanes]
        store(split_ref.at[offset], piece)
    copies[1].wait()
    for offset, piece in enumerate(query_refs):
        size = positions // sets
        first = lax.rem(me + offset, sets) * size
        store(held_ref.at[1, pl.ds(pl.multiple_of(first, size), size)], piece)
    for slot in (0, 1):
        copies[2 + slot].wait()
        turned = held_ref[2 + slot].astype(F32).T
        turned_ref[slot] = turned.reshape(count, rows, positions).astype(BF16)
        store(turned_ref.at[slot], sent_ref.at[:, slot])
    for result in results:
        result.wait()


def heads_kernel(sets, *refs):
    parts, pieces = refs[:sets], refs[sets:]
    head_dim = pieces[0].shape[2]
    mine = lax.axis_index("seq") // sets
    for offset, piece in enumerate(pieces):
        head = lax.rem(mine + offset, len(pieces))
        lanes = pl.ds(pl.multiple_of(head * head_dim, head_dim), head_dim)
        for index, part in enumerate(parts):
            piece[index] = part[:, lanes]


def join_kernel(count, *refs):
    pieces, (joined_ref, semaphores) = refs[:count], refs[-2:]
    copies = [
        pltpu.make_async_copy(piece, joined_ref.at[index], semaphores.at[index])
        for index, piece in enumerate(pieces)
    ]
    for copy in copies:
        copy.start()
    for copy in copies:
        copy.wait()


def squares_kernel(rows, home_ref, after_ref, squares_ref):
    squares_ref[...] = jnp.sum(home_ref[:, rows:].astype(F32), axis=0)


def arrange_kernel(sets, *refs):
    key_parts, query_parts, (keys_ref, queries_ref, semaphores) = refs[:sets], refs[sets:-3], refs[-3:]
    heads = len(query_parts)
    me = lax.axis_index("seq")
    copies = []
    for index in range(heads):
        for offset in range(sets):
            source = lax.rem(me // sets + heads - index, heads) * sets + lax.rem(me + offset, sets)
            for slot, (part, target) in enumerate((
                (key_parts[offset].at[index], keys_ref.at[source]),
                (query_parts[index].at[offset], queries_ref.at[source]),
            )):
                semaphore = semaphores.at[slot, offset, index]
                copies.append(pltpu.make_async_copy(part, target, semaphore))
    for copy in copies:
        copy.start()
    for copy in copies:
        copy.wait()


def unpack_kernel(got_ref, out_ref):
    count = got_ref.shape[0]
    rows = out_ref.shape[1] // count
    whole = got_ref[:, :rows].astype(F32).reshape(count * rows, got_ref.shape[2])
    out_ref[...] = whole.T.astype(BF16)


def toeplitz_kernel(head_count_per, taps_ref, matrix_ref):
    block, length = matrix_ref.shape
    head = lax.axis_index("seq") // head_count_per
    taps = taps_ref[...].astype(F32)
    mine = lax.broadcasted_iota(jnp.int32, taps.shape, 0) == head
    row = jnp.sum(jnp.where(mine, taps, 0.0), axis=0, keepdims=True)
    rolled = pltpu.roll(jnp.broadcast_to(row, (block, length)), 0, 1, stride=1, stride_axis=0)
    source = lax.broadcasted_iota(jnp.int32, (block, block), 0)
    target = lax.broadcasted_iota(jnp.int32, (block, block), 1)
    matrix_ref[:, :block] = jnp.where(target >= source, rolled[:, :block], 0.0).astype(BF16)
    matrix_ref[:, block:] = rolled[:, block:].astype(BF16)


def conv_kernel(got_ref, matrix_ref, skip_ref, mixed_ref, back_ref, total_ref):
    count, _, rows, block = got_ref.shape
    inputs = merge_rows(got_ref[:, 0])
    before = jnp.concatenate([jnp.zeros((rows, block), BF16), inputs[: (count - 1) * rows]], axis=0)
    pairs = jnp.concatenate([inputs, before], axis=1)
    for lag in range(0, count, 2):
        spans = [slice((lag + more) * block, (lag + more + 1) * block) for more in (0, 1)]
        product = jnp.dot(
            pairs[: (count - lag) * rows],
            jnp.concatenate([matrix_ref[:, span] for span in spans], axis=0),
            preferred_element_type=F32,
        )
        if lag == 0:
            total_ref[...] = product
        else:
            total_ref[lag * rows :] += product
    skip = skip_ref[...]
    sums = []
    for index in range(count):
        conv = total_ref[index * rows : (index + 1) * rows]
        direct = skip * got_ref[index, 0].astype(F32)
        mixed = (got_ref[index, 1].astype(F32) * (conv + direct)).astype(BF16)
        mixed_ref[index] = mixed
        back_ref[index, :rows] = mixed
        widened = mixed.astype(F32)
        sums.append(jnp.sum(widened * widened, axis=0, keepdims=True))
    squares = jnp.concatenate(sums, axis=0)
    both = squares.astype(BF16)
    for index in range(count):
        back_ref[index, rows:] = both


def weights_block(step, last, key_ref, query, sets, rows, scores_ref, weights_ref, total_ref):
    wide = query.shape[0]
    seq_block = sets * rows
    reach = wide // rows * seq_block
    chunk = min(KEY_CHUNK, reach)
    chunks = (step + 1) * reach // chunk
    head_dim = query.shape[1]
    factor = math.log2(math.e) / math.sqrt(head_dim)
    mine = lax.rem(lax.axis_index("seq"), sets)
    lane = step * wide + lax.broadcasted_iota(jnp.int32, (1, wide), 1)
    query_pos = lane // rows * seq_block + mine * rows + lax.rem(lane, rows)

    def score(index, peak):
        first = index * chunk
        part = key_ref[pl.ds(first, chunk), :]
        raw = lax.dot_general(part, query, NT, preferred_element_type=F32)
        if not isinstance(index, int) or first + chunk - 1 > step * reach:
            key_pos = first + lax.broadcasted_iota(jnp.int32, (chunk, 1), 0)
            raw = jnp.where(key_pos <= query_pos, raw, -jnp.inf)
        scores_ref[pl.ds(first, chunk), :] = raw
        return jnp.maximum(peak, jnp.max(raw, axis=0, keepdims=True))

    peak = loop(chunks, score, jnp.full((1, wide), -jnp.inf, F32))

    def weigh(index, total):
        first = index * chunk
        weights = jnp.exp2((scores_ref[pl.ds(first, chunk), :] - peak) * factor)
        weights_ref[pl.ds(first, chunk), :] = weights.astype(BF16)
        return total + jnp.sum(weights, axis=0, keepdims=True)

    total = loop(chunks, weigh, jnp.zeros((1, wide), F32))
    total_ref[...] = jnp.broadcast_to(1.0 / total, total_ref.shape)


def weights_kernel(gridded, key_ref, query_ref, total_ref, *refs):
    weights_refs, scores_ref = refs[:-1], refs[-1]
    count, positions, head_dim = key_ref.shape
    rows = query_ref.shape[1]
    sets = positions // rows
    steps = count * rows // QUERY_BLOCK
    keys = key_ref.reshape(count * positions, head_dim)

    def block(step, weights, total):
        each = QUERY_BLOCK // rows
        query = merge_rows(query_ref[step * each : (step + 1) * each])
        weights_block(step, steps - 1, keys, query, sets, rows, scores_ref, weights, total)

    if not gridded:
        for step in range(steps):
            block(step, weights_refs[step], total_ref.at[step])
        return
    for step in range(steps):
        pl.when(pl.program_id(0) == step)(
            functools.partial(block, step, weights_refs[0].at[0], total_ref.at[0])
        )


def output_kernel(sets, steps, width, gridded, *refs):
    own = 4 if gridded else 6
    first = len(refs) - own - sets - (1 if gridded else steps)
    squares_refs, parts, refs = refs[:first], refs[first : first + sets], refs[first + sets :]
    total_ref, weights_refs, refs = refs[0], refs[1 : 1 - own], refs[1 - own :]
    out_ref, wide_ref, values_ref = refs[:3]
    count, rows, block = parts[0].shape
    mine = lax.rem(lax.axis_index("seq"), sets)
    reach = count * block // steps

    def norm():
        squares = sum(ref[...] for ref in squares_refs[1:]) + squares_refs[0][...]
        inv_scale = lax.rsqrt(squares / width + 1e-06)
        for offset in range(sets):
            place = lax.rem(mine + offset, sets)
            for index in range(count):
                span = slice(index * block, (index + 1) * block)
                part = parts[offset][index].astype(F32) * inv_scale[index : index + 1]
                if rows % 16:
                    wide_ref[place, :, span] = part
                else:
                    lines = pl.ds(pl.multiple_of(place * rows, rows), rows)
                    values_ref[lines, span] = part.astype(BF16)
        if rows % 16:
            for index in range(count):
                span = slice(index * block, (index + 1) * block)
                values_ref[:, span] = merge_rows(wide_ref[:, :, span]).astype(BF16)

    def attend(step, weights, total):
        keys = (step + 1) * reach
        summed = jnp.dot(values_ref[:, :keys], weights[:keys], preferred_element_type=F32)
        return (summed * total[:1]).T.astype(BF16)

    if gridded:
        pl.when(pl.program_id(0) == 0)(norm)

        def block_of(step):
            out_ref[...] = attend(step, weights_refs[0].at[0], total_ref.at[0])

        for step in range(steps):
            pl.when(pl.program_id(0) == step)(functools.partial(block_of, step))
        return
    staged_ref, semaphores = refs[3:]
    norm()
    copies = []
    for step in reversed(range(steps)):
        staged_ref[step] = attend(step, weights_refs[step], total_ref.at[step])
        lines = out_ref.at[pl.ds(step * QUERY_BLOCK, QUERY_BLOCK)]
        copies.append(pltpu.make_async_copy(staged_ref.at[step], lines, semaphores.at[step]))
        copies[-1].start()
    for copy in copies:
        copy.wait()


def shards(signal, gate_rows, skip_gain, filter_taps, queries, key_rows):
    block, local_width = signal.shape
    heads_loc = filter_taps.shape[1]
    head_dim = local_width // heads_loc
    seq_count = lax.axis_size("seq")
    chan_count = lax.axis_size("chan")
    everyone = seq_count * chan_count
    length = block * seq_count
    sets = seq_count // heads_loc
    rows = block // sets
    channels = local_width // seq_count
    query_len = length // sets
    steps = query_len // QUERY_BLOCK
    gridded = length > 4096
    shape = jax.ShapeDtypeStruct

    def from_set(array, offset):
        pairs = []
        for head in range(heads_loc):
            for part in range(sets):
                pairs.append((head * sets + (part + offset) % sets, head * sets + part))
        return lax.ppermute(array, "seq", pairs)

    def from_head(array, offset):
        pairs = [(source, (source + offset * sets) % seq_count) for source in range(seq_count)]
        return lax.ppermute(array, "seq", pairs)

    anywhere = pl.BlockSpec(memory_space=pl.ANY)
    packed, *pieces = call(
        functools.partial(pack_kernel, sets, heads_loc),
        [shape((seq_count, 2, channels, block), BF16)]
        + [shape((block, head_dim), BF16)] * heads_loc
        + [shape((rows, local_width), BF16)] * sets,
        moved=16 * signal.size,
        in_specs=[anywhere] * 4,
        out_specs=[anywhere] * (1 + heads_loc + sets),
        vmem=56,
        scratch_shapes=[
            pltpu.VMEM((4,) + signal.shape, BF16),
            pltpu.VMEM((heads_loc, block, head_dim), BF16),
            pltpu.VMEM((2, seq_count, channels, block), BF16),
            pltpu.SemaphoreType.DMA((4,)),
            pltpu.SemaphoreType.DMA((heads_loc + sets + 2,)),
        ],
    )(signal, gate_rows, queries, key_rows)
    got = lax.all_to_all(packed, "seq", 0, 0, tiled=True)
    key_pieces, set_queries = pieces[:heads_loc], pieces[heads_loc:]
    key_pieces = key_pieces[:1] + [from_head(key_pieces[k], k) for k in range(1, heads_loc)]
    matrix = call(
        functools.partial(toeplitz_kernel, sets),
        shape((block, length), BF16),
        moved=block * length * 2,
        flops=block * length * 8,
        vmem=8 if not gridded else 56,
    )(filter_taps.T)
    skip = lax.dynamic_slice_in_dim(skip_gain, lax.axis_index("seq") * channels, channels)[:, None]

    whole = pl.BlockSpec(memory_space=pltpu.VMEM)
    own_keys = call(
        functools.partial(join_kernel, heads_loc),
        shape((heads_loc, block, head_dim), BF16),
        moved=4 * signal.size,
        flops=4 * 10**10,
        in_specs=[anywhere] * (heads_loc + 1),
        out_specs=anywhere,
        scratch_shapes=[pltpu.SemaphoreType.DMA((heads_loc,))],
    )(*key_pieces, matrix)
    key_parts = [own_keys] + [from_set(own_keys, k) for k in range(1, sets)]
    query_sets = set_queries[:1] + [from_set(set_queries[-k], k) for k in range(1, sets)]
    query_pieces = call(
        functools.partial(heads_kernel, sets),
        [shape((sets, rows, head_dim), BF16)] * heads_loc,
        moved=4 * signal.size,
        flops=0,
    )(*query_sets)
    query_parts = [query_pieces[0]] + [from_head(query_pieces[k], k) for k in range(1, heads_loc)]

    mixed, back = call(
        conv_kernel,
        [
            shape((seq_count, channels, block), BF16),
            shape((seq_count, channels + seq_count, block), BF16),
        ],
        moved=signal.size * 10,
        flops=length * length * channels,
        vmem=8 if not gridded else 56,
        scratch_shapes=[pltpu.VMEM((seq_count * channels, block), F32)],
    )(got, matrix, skip)

    home = lax.all_to_all(back, "seq", 0, 0, tiled=True)
    mixed_parts = [mixed] + [from_set(mixed, offset) for offset in range(1, sets)]
    total_shape = (steps, 8, QUERY_BLOCK)
    one = lambda dims: pl.BlockSpec((1,) + dims[1:], lambda step: (step, 0, 0))
    whole = pl.BlockSpec(memory_space=pltpu.VMEM)
    if gridded:
        weights_shapes = [(steps, length, QUERY_BLOCK)]
        vmem = 56
        weights_specs = [one(total_shape), one(weights_shapes[0])]
        weights_grid = dict(grid=(steps,), in_specs=[whole] * 2, out_specs=weights_specs)
        output_grid = dict(
            grid=(steps,),
            in_specs=[whole] * (chan_count + sets) + weights_specs,
            out_specs=pl.BlockSpec((QUERY_BLOCK, head_dim), lambda step: (step, 0)),
        )
    else:
        weights_shapes = [(length * step // steps, QUERY_BLOCK) for step in range(1, steps + 1)]
        vmem = 12
        weights_grid = {}
        output_grid = dict(
            in_specs=[whole] * (chan_count + sets + 1 + steps),
            out_specs=anywhere,
        )
        output_scratch = [
            pltpu.VMEM((steps, QUERY_BLOCK, head_dim), BF16),
            pltpu.SemaphoreType.DMA((steps,)),
        ]
    keys, arranged = call(
        functools.partial(arrange_kernel, sets),
        [shape((seq_count, block, head_dim), BF16), shape((seq_count, rows, head_dim), BF16)],
        moved=6 * length * head_dim,
        flops=4 * 10**10,
        in_specs=[anywhere] * (sets + heads_loc),
        out_specs=[anywhere] * 2,
        scratch_shapes=[pltpu.SemaphoreType.DMA((2, sets, heads_loc))],
    )(*key_parts, *query_parts)
    totals, *weights = call(
        functools.partial(weights_kernel, gridded),
        [shape(total_shape, F32)] + [shape(dims, BF16) for dims in weights_shapes],
        moved=2 * sum(math.prod(dims) for dims in weights_shapes),
        flops=query_len * length * head_dim,
        exps=query_len * length // 2,
        vmem=vmem,
        scratch_shapes=[
            pltpu.VMEM((length, QUERY_BLOCK), F32),
        ],
        **weights_grid,
    )(keys, arranged)

    squares = call(
        functools.partial(squares_kernel, channels),
        shape((seq_count, block), F32),
        moved=4 * length,
        in_specs=[whole, anywhere],
        vmem=8 if not gridded else 56,
    )(home, totals)
    all_squares = [squares]
    for offset in range(1, chan_count):
        pairs = [(source, (source + offset) % chan_count) for source in range(chan_count)]
        all_squares.append(lax.ppermute(squares, "chan", pairs))

    attended = call(
        functools.partial(output_kernel, sets, steps, local_width * chan_count, gridded),
        shape((query_len, head_dim), BF16),
        moved=2 * sum(math.prod(dims) for dims in weights_shapes),
        flops=query_len * length * head_dim,
        vmem=vmem,
        scratch_shapes=[
            pltpu.VMEM((sets, channels, length if channels % 16 else block), F32),
            pltpu.VMEM((head_dim, length), BF16),
        ]
        + ([] if gridded else output_scratch),
        **output_grid,
    )(*all_squares, *mixed_parts, totals, *weights)

    conv_mixed = call(unpack_kernel, shape((block, local_width), BF16), moved=signal.size * 4)(home)
    return (conv_mixed, attended[None])


def solution(mesh):
    in_specs = (
        P("seq", "chan"),
        P("seq", "chan"),
        P("chan"),
        P(None, "chan"),
        P("seq", "chan"),
        P("seq", "chan"),
    )
    out_specs = (P("seq", "chan"), P(("chan", "seq"), None, None))
    return jax.shard_map(shards, mesh=mesh, in_specs=in_specs, out_specs=out_specs, check_vma=False)
```

```python
import functools
import math

import jax
import jax.numpy as jnp
from jax import lax
from jax.experimental import pallas as pl
from jax.experimental.pallas import tpu as pltpu
from jax.sharding import PartitionSpec as P

BF16, F32 = jnp.bfloat16, jnp.float32
QUERY_BLOCK = 256
KEY_CHUNK = 512
NT = (((1,), (1,)), ((), ()))


def call(kernel, out_shape, flops=0, exps=0, moved=0, vmem=8, **options):
    return pl.pallas_call(
        kernel,
        out_shape=out_shape,
        compiler_params=pltpu.CompilerParams(vmem_limit_bytes=vmem * 1024 * 1024),
        cost_estimate=pl.CostEstimate(flops=flops, bytes_accessed=moved, transcendentals=exps),
        **options,
    )


def merge_rows(blocks):
    count, rows, columns = blocks.shape
    if blocks.dtype == BF16 and rows % 16:
        return blocks.astype(F32).reshape(count * rows, columns).astype(BF16)
    return blocks.reshape(count * rows, columns)


def loop(count, body, carry):
    if count <= 8:
        for index in range(count):
            carry = body(index, carry)
        return carry
    return lax.fori_loop(0, count, body, carry)


def pack_kernel(sets, heads, signal_ref, gate_ref, query_ref, key_ref, *refs):
    sent_ref, key_refs, query_refs = refs[0], refs[1 : 1 + heads], refs[1 + heads : 1 + heads + sets]
    held_ref, split_ref, turned_ref, loads, stores = refs[1 + heads + sets :]
    _, count, rows, positions = turned_ref.shape
    head_dim = split_ref.shape[2]
    copies = [
        pltpu.make_async_copy(source, held_ref.at[slot], loads.at[slot])
        for slot, source in enumerate((key_ref, query_ref, signal_ref, gate_ref))
    ]
    for copy in copies:
        copy.start()
    me = lax.axis_index("seq")
    results = []

    def store(source, target):
        results.append(pltpu.make_async_copy(source, target, stores.at[len(results)]))
        results[-1].start()

    copies[0].wait()
    for offset, piece in enumerate(key_refs):
        head = lax.rem(me // sets + offset, heads)
        lanes = pl.ds(pl.multiple_of(head * head_dim, head_dim), head_dim)
        split_ref[offset] = held_ref[0, :, lanes]
        store(split_ref.at[offset], piece)
    copies[1].wait()
    for offset, piece in enumerate(query_refs):
        size = positions // sets
        first = lax.rem(me + offset, sets) * size
        store(held_ref.at[1, pl.ds(pl.multiple_of(first, size), size)], piece)
    for slot in (0, 1):
        copies[2 + slot].wait()
        turned = held_ref[2 + slot].astype(F32).T
        turned_ref[slot] = turned.reshape(count, rows, positions).astype(BF16)
        store(turned_ref.at[slot], sent_ref.at[:, slot])
    for result in results:
        result.wait()


def heads_kernel(sets, *refs):
    parts, pieces = refs[:sets], refs[sets:]
    head_dim = pieces[0].shape[2]
    mine = lax.axis_index("seq") // sets
    for offset, piece in enumerate(pieces):
        head = lax.rem(mine + offset, len(pieces))
        lanes = pl.ds(pl.multiple_of(head * head_dim, head_dim), head_dim)
        for index, part in enumerate(parts):
            piece[index] = part[:, lanes]


def join_kernel(count, *refs):
    pieces, (joined_ref, semaphores) = refs[:count], refs[-2:]
    copies = [
        pltpu.make_async_copy(piece, joined_ref.at[index], semaphores.at[index])
        for index, piece in enumerate(pieces)
    ]
    for copy in copies:
        copy.start()
    for copy in copies:
        copy.wait()


def squares_kernel(rows, home_ref, after_ref, squares_ref):
    squares_ref[...] = jnp.sum(home_ref[:, rows:].astype(F32), axis=0)


def arrange_kernel(sets, *refs):
    key_parts, query_parts, (keys_ref, queries_ref, semaphores) = refs[:sets], refs[sets:-3], refs[-3:]
    heads = len(query_parts)
    me = lax.axis_index("seq")
    copies = []
    for index in range(heads):
        for offset in range(sets):
            source = lax.rem(me // sets + heads - index, heads) * sets + lax.rem(me + offset, sets)
            for slot, (part, target) in enumerate((
                (key_parts[offset].at[index], keys_ref.at[source]),
                (query_parts[index].at[offset], queries_ref.at[source]),
            )):
                semaphore = semaphores.at[slot, offset, index]
                copies.append(pltpu.make_async_copy(part, target, semaphore))
    for copy in copies:
        copy.start()
    for copy in copies:
        copy.wait()


def unpack_kernel(got_ref, out_ref):
    count = got_ref.shape[0]
    rows = out_ref.shape[1] // count
    whole = got_ref[:, :rows].astype(F32).reshape(count * rows, got_ref.shape[2])
    out_ref[...] = whole.T.astype(BF16)


def toeplitz_kernel(head_count_per, taps_ref, matrix_ref):
    block, length = matrix_ref.shape
    head = lax.axis_index("seq") // head_count_per
    taps = taps_ref[...].astype(F32)
    mine = lax.broadcasted_iota(jnp.int32, taps.shape, 0) == head
    row = jnp.sum(jnp.where(mine, taps, 0.0), axis=0, keepdims=True)
    rolled = pltpu.roll(jnp.broadcast_to(row, (block, length)), 0, 1, stride=1, stride_axis=0)
    source = lax.broadcasted_iota(jnp.int32, (block, block), 0)
    target = lax.broadcasted_iota(jnp.int32, (block, block), 1)
    matrix_ref[:, :block] = jnp.where(target >= source, rolled[:, :block], 0.0).astype(BF16)
    matrix_ref[:, block:] = rolled[:, block:].astype(BF16)


def conv_kernel(got_ref, matrix_ref, skip_ref, mixed_ref, back_ref, total_ref):
    count, _, rows, block = got_ref.shape
    inputs = merge_rows(got_ref[:, 0])
    before = jnp.concatenate([jnp.zeros((rows, block), BF16), inputs[: (count - 1) * rows]], axis=0)
    pairs = jnp.concatenate([inputs, before], axis=1)
    for lag in range(0, count, 2):
        spans = [slice((lag + more) * block, (lag + more + 1) * block) for more in (0, 1)]
        product = jnp.dot(
            pairs[: (count - lag) * rows],
            jnp.concatenate([matrix_ref[:, span] for span in spans], axis=0),
            preferred_element_type=F32,
        )
        if lag == 0:
            total_ref[...] = product
        else:
            total_ref[lag * rows :] += product
    skip = skip_ref[...]
    sums = []
    for index in range(count):
        conv = total_ref[index * rows : (index + 1) * rows]
        direct = skip * got_ref[index, 0].astype(F32)
        mixed = (got_ref[index, 1].astype(F32) * (conv + direct)).astype(BF16)
        mixed_ref[index] = mixed
        back_ref[index, :rows] = mixed
        widened = mixed.astype(F32)
        sums.append(jnp.sum(widened * widened, axis=0, keepdims=True))
    squares = jnp.concatenate(sums, axis=0)
    both = squares.astype(BF16)
    for index in range(count):
        back_ref[index, rows:] = both


def weights_block(step, last, key_ref, query, sets, rows, scores_ref, weights_ref, total_ref):
    wide = query.shape[0]
    seq_block = sets * rows
    reach = wide // rows * seq_block
    chunk = min(KEY_CHUNK, reach)
    chunks = (step + 1) * reach // chunk
    head_dim = query.shape[1]
    factor = math.log2(math.e) / math.sqrt(head_dim)
    mine = lax.rem(lax.axis_index("seq"), sets)
    lane = step * wide + lax.broadcasted_iota(jnp.int32, (1, wide), 1)
    query_pos = lane // rows * seq_block + mine * rows + lax.rem(lane, rows)

    def score(index, peak):
        first = index * chunk
        part = key_ref[pl.ds(first, chunk), :]
        raw = lax.dot_general(part, query, NT, preferred_element_type=F32)
        if not isinstance(index, int) or first + chunk - 1 > step * reach:
            key_pos = first + lax.broadcasted_iota(jnp.int32, (chunk, 1), 0)
            raw = jnp.where(key_pos <= query_pos, raw, -jnp.inf)
        scores_ref[pl.ds(first, chunk), :] = raw
        return jnp.maximum(peak, jnp.max(raw, axis=0, keepdims=True))

    peak = loop(chunks, score, jnp.full((1, wide), -jnp.inf, F32))

    def weigh(index, total):
        first = index * chunk
        weights = jnp.exp2((scores_ref[pl.ds(first, chunk), :] - peak) * factor)
        weights_ref[pl.ds(first, chunk), :] = weights.astype(BF16)
        return total + jnp.sum(weights, axis=0, keepdims=True)

    total = loop(chunks, weigh, jnp.zeros((1, wide), F32))
    total_ref[...] = jnp.broadcast_to(1.0 / total, total_ref.shape)


def weights_kernel(gridded, key_ref, query_ref, total_ref, *refs):
    weights_refs, scores_ref = refs[:-1], refs[-1]
    count, positions, head_dim = key_ref.shape
    rows = query_ref.shape[1]
    sets = positions // rows
    steps = count * rows // QUERY_BLOCK
    keys = key_ref.reshape(count * positions, head_dim)

    def block(step, weights, total):
        each = QUERY_BLOCK // rows
        query = merge_rows(query_ref[step * each : (step + 1) * each])
        weights_block(step, steps - 1, keys, query, sets, rows, scores_ref, weights, total)

    if not gridded:
        for step in range(steps):
            block(step, weights_refs[step], total_ref.at[step])
        return
    for step in range(steps):
        pl.when(pl.program_id(0) == step)(
            functools.partial(block, step, weights_refs[0].at[0], total_ref.at[0])
        )


def output_kernel(sets, steps, width, gridded, *refs):
    own = 4 if gridded else 6
    first = len(refs) - own - sets - (1 if gridded else steps)
    squares_refs, parts, refs = refs[:first], refs[first : first + sets], refs[first + sets :]
    total_ref, weights_refs, refs = refs[0], refs[1 : 1 - own], refs[1 - own :]
    out_ref, wide_ref, values_ref = refs[:3]
    count, rows, block = parts[0].shape
    mine = lax.rem(lax.axis_index("seq"), sets)
    reach = count * block // steps

    def norm():
        squares = sum(ref[...] for ref in squares_refs[1:]) + squares_refs[0][...]
        inv_scale = lax.rsqrt(squares / width + 1e-06)
        for offset in range(sets):
            place = lax.rem(mine + offset, sets)
            for index in range(count):
                span = slice(index * block, (index + 1) * block)
                part = parts[offset][index].astype(F32) * inv_scale[index : index + 1]
                if rows % 16:
                    wide_ref[place, :, span] = part
                else:
                    lines = pl.ds(pl.multiple_of(place * rows, rows), rows)
                    values_ref[lines, span] = part.astype(BF16)
        if rows % 16:
            for index in range(count):
                span = slice(index * block, (index + 1) * block)
                values_ref[:, span] = merge_rows(wide_ref[:, :, span]).astype(BF16)

    def attend(step, weights, total):
        keys = (step + 1) * reach
        summed = jnp.dot(values_ref[:, :keys], weights[:keys], preferred_element_type=F32)
        return (summed * total[:1]).T.astype(BF16)

    if gridded:
        pl.when(pl.program_id(0) == 0)(norm)

        def block_of(step):
            out_ref[...] = attend(step, weights_refs[0].at[0], total_ref.at[0])

        for step in range(steps):
            pl.when(pl.program_id(0) == step)(functools.partial(block_of, step))
        return
    staged_ref, semaphores = refs[3:]
    norm()
    copies = []
    for step in reversed(range(steps)):
        staged_ref[step] = attend(step, weights_refs[step], total_ref.at[step])
        lines = out_ref.at[pl.ds(step * QUERY_BLOCK, QUERY_BLOCK)]
        copies.append(pltpu.make_async_copy(staged_ref.at[step], lines, semaphores.at[step]))
        copies[-1].start()
    for copy in copies:
        copy.wait()


def shards(signal, gate_rows, skip_gain, filter_taps, queries, key_rows):
    block, local_width = signal.shape
    heads_loc = filter_taps.shape[1]
    head_dim = local_width // heads_loc
    seq_count = lax.axis_size("seq")
    chan_count = lax.axis_size("chan")
    everyone = seq_count * chan_count
    length = block * seq_count
    sets = seq_count // heads_loc
    rows = block // sets
    channels = local_width // seq_count
    query_len = length // sets
    steps = query_len // QUERY_BLOCK
    gridded = length > 4096
    shape = jax.ShapeDtypeStruct

    def from_set(array, offset):
        pairs = []
        for head in range(heads_loc):
            for part in range(sets):
                pairs.append((head * sets + (part + offset) % sets, head * sets + part))
        return lax.ppermute(array, "seq", pairs)

    def from_head(array, offset):
        pairs = [(source, (source + offset * sets) % seq_count) for source in range(seq_count)]
        return lax.ppermute(array, "seq", pairs)

    anywhere = pl.BlockSpec(memory_space=pl.ANY)
    packed, *pieces = call(
        functools.partial(pack_kernel, sets, heads_loc),
        [shape((seq_count, 2, channels, block), BF16)]
        + [shape((block, head_dim), BF16)] * heads_loc
        + [shape((rows, local_width), BF16)] * sets,
        moved=16 * signal.size,
        in_specs=[anywhere] * 4,
        out_specs=[anywhere] * (1 + heads_loc + sets),
        vmem=56,
        scratch_shapes=[
            pltpu.VMEM((4,) + signal.shape, BF16),
            pltpu.VMEM((heads_loc, block, head_dim), BF16),
            pltpu.VMEM((2, seq_count, channels, block), BF16),
            pltpu.SemaphoreType.DMA((4,)),
            pltpu.SemaphoreType.DMA((heads_loc + sets + 2,)),
        ],
    )(signal, gate_rows, queries, key_rows)
    got = lax.all_to_all(packed, "seq", 0, 0, tiled=True)
    key_pieces, set_queries = pieces[:heads_loc], pieces[heads_loc:]
    key_pieces = key_pieces[:1] + [from_head(key_pieces[k], k) for k in range(1, heads_loc)]
    matrix = call(
        functools.partial(toeplitz_kernel, sets),
        shape((block, length), BF16),
        moved=block * length * 2,
        flops=block * length * 8,
        vmem=8 if not gridded else 56,
    )(filter_taps.T)
    skip = lax.dynamic_slice_in_dim(skip_gain, lax.axis_index("seq") * channels, channels)[:, None]

    whole = pl.BlockSpec(memory_space=pltpu.VMEM)
    own_keys = call(
        functools.partial(join_kernel, heads_loc),
        shape((heads_loc, block, head_dim), BF16),
        moved=4 * signal.size,
        flops=4 * 10**10,
        in_specs=[anywhere] * (heads_loc + 1),
        out_specs=anywhere,
        scratch_shapes=[pltpu.SemaphoreType.DMA((heads_loc,))],
    )(*key_pieces, matrix)
    key_parts = [own_keys] + [from_set(own_keys, k) for k in range(1, sets)]
    query_sets = set_queries[:1] + [from_set(set_queries[-k], k) for k in range(1, sets)]
    query_pieces = call(
        functools.partial(heads_kernel, sets),
        [shape((sets, rows, head_dim), BF16)] * heads_loc,
        moved=4 * signal.size,
        flops=0,
    )(*query_sets)
    query_parts = [query_pieces[0]] + [from_head(query_pieces[k], k) for k in range(1, heads_loc)]

    mixed, back = call(
        conv_kernel,
        [
            shape((seq_count, channels, block), BF16),
            shape((seq_count, channels + seq_count, block), BF16),
        ],
        moved=signal.size * 10,
        flops=length * length * channels,
        vmem=8 if not gridded else 56,
        scratch_shapes=[pltpu.VMEM((seq_count * channels, block), F32)],
    )(got, matrix, skip)

    home = lax.all_to_all(back, "seq", 0, 0, tiled=True)
    mixed_parts = [mixed] + [from_set(mixed, offset) for offset in range(1, sets)]
    total_shape = (steps, 8, QUERY_BLOCK)
    one = lambda dims: pl.BlockSpec((1,) + dims[1:], lambda step: (step, 0, 0))
    whole = pl.BlockSpec(memory_space=pltpu.VMEM)
    if gridded:
        weights_shapes = [(steps, length, QUERY_BLOCK)]
        vmem = 56
        weights_specs = [one(total_shape), one(weights_shapes[0])]
        weights_grid = dict(grid=(steps,), in_specs=[whole] * 2, out_specs=weights_specs)
        output_grid = dict(
            grid=(steps,),
            in_specs=[whole] * (chan_count + sets) + weights_specs,
            out_specs=pl.BlockSpec((QUERY_BLOCK, head_dim), lambda step: (step, 0)),
        )
    else:
        weights_shapes = [(length * step // steps, QUERY_BLOCK) for step in range(1, steps + 1)]
        vmem = 12
        weights_grid = {}
        output_grid = dict(
            in_specs=[whole] * (chan_count + sets + 1 + steps),
            out_specs=anywhere,
        )
        output_scratch = [
            pltpu.VMEM((steps, QUERY_BLOCK, head_dim), BF16),
            pltpu.SemaphoreType.DMA((steps,)),
        ]
    keys, arranged = call(
        functools.partial(arrange_kernel, sets),
        [shape((seq_count, block, head_dim), BF16), shape((seq_count, rows, head_dim), BF16)],
        moved=6 * length * head_dim,
        flops=4 * 10**10,
        in_specs=[anywhere] * (sets + heads_loc),
        out_specs=[anywhere] * 2,
        scratch_shapes=[pltpu.SemaphoreType.DMA((2, sets, heads_loc))],
    )(*key_parts, *query_parts)
    totals, *weights = call(
        functools.partial(weights_kernel, gridded),
        [shape(total_shape, F32)] + [shape(dims, BF16) for dims in weights_shapes],
        moved=2 * sum(math.prod(dims) for dims in weights_shapes),
        flops=query_len * length * head_dim,
        exps=query_len * length // 2,
        vmem=vmem,
        scratch_shapes=[
            pltpu.VMEM((length, QUERY_BLOCK), F32),
        ],
        **weights_grid,
    )(keys, arranged)

    squares = call(
        functools.partial(squares_kernel, channels),
        shape((seq_count, block), F32),
        moved=4 * length,
        in_specs=[whole, anywhere],
        vmem=8 if not gridded else 56,
    )(home, totals)
    all_squares = [squares]
    for offset in range(1, chan_count):
        pairs = [(source, source ^ offset) for source in range(chan_count)]
        all_squares.append(lax.ppermute(squares, "chan", pairs))

    attended = call(
        functools.partial(output_kernel, sets, steps, local_width * chan_count, gridded),
        shape((query_len, head_dim), BF16),
        moved=2 * sum(math.prod(dims) for dims in weights_shapes),
        flops=query_len * length * head_dim,
        vmem=vmem,
        scratch_shapes=[
            pltpu.VMEM((sets, channels, length if channels % 16 else block), F32),
            pltpu.VMEM((head_dim, length), BF16),
        ]
        + ([] if gridded else output_scratch),
        **output_grid,
    )(*all_squares, *mixed_parts, totals, *weights)

    conv_mixed = call(unpack_kernel, shape((block, local_width), BF16), moved=signal.size * 4)(home)
    return (conv_mixed, attended[None])


def solution(mesh):
    in_specs = (
        P("seq", "chan"),
        P("seq", "chan"),
        P("chan"),
        P(None, "chan"),
        P("seq", "chan"),
        P("seq", "chan"),
    )
    out_specs = (P("seq", "chan"), P(("chan", "seq"), None, None))
    return jax.shard_map(shards, mesh=mesh, in_specs=in_specs, out_specs=out_specs, check_vma=False)
```

```python
import functools
import math

import jax
import jax.numpy as jnp
from jax import lax
from jax.experimental import pallas as pl
from jax.experimental.pallas import tpu as pltpu
from jax.sharding import PartitionSpec as P

BF16, F32 = jnp.bfloat16, jnp.float32
QUERY_BLOCK = 256
KEY_CHUNK = 512
NT = (((1,), (1,)), ((), ()))


def call(kernel, out_shape, flops=0, exps=0, moved=0, vmem=8, **options):
    return pl.pallas_call(
        kernel,
        out_shape=out_shape,
        compiler_params=pltpu.CompilerParams(vmem_limit_bytes=vmem * 1024 * 1024),
        cost_estimate=pl.CostEstimate(flops=flops, bytes_accessed=moved, transcendentals=exps),
        **options,
    )


def merge_rows(blocks):
    count, rows, columns = blocks.shape
    if blocks.dtype == BF16 and rows % 16:
        return blocks.astype(F32).reshape(count * rows, columns).astype(BF16)
    return blocks.reshape(count * rows, columns)


def loop(count, body, carry):
    if count <= 8:
        for index in range(count):
            carry = body(index, carry)
        return carry
    return lax.fori_loop(0, count, body, carry)


def pack_kernel(sets, heads, signal_ref, gate_ref, query_ref, key_ref, *refs):
    sent_ref, key_refs, query_refs = refs[0], refs[1 : 1 + heads], refs[1 + heads : 1 + heads + sets]
    held_ref, split_ref, turned_ref, loads, stores = refs[1 + heads + sets :]
    _, count, rows, positions = turned_ref.shape
    head_dim = split_ref.shape[2]
    copies = [
        pltpu.make_async_copy(source, held_ref.at[slot], loads.at[slot])
        for slot, source in enumerate((key_ref, query_ref, signal_ref, gate_ref))
    ]
    for copy in copies:
        copy.start()
    me = lax.axis_index("seq")
    results = []

    def store(source, target):
        results.append(pltpu.make_async_copy(source, target, stores.at[len(results)]))
        results[-1].start()

    copies[0].wait()
    for offset, piece in enumerate(key_refs):
        head = lax.rem(me // sets + offset, heads)
        lanes = pl.ds(pl.multiple_of(head * head_dim, head_dim), head_dim)
        split_ref[offset] = held_ref[0, :, lanes]
        store(split_ref.at[offset], piece)
    copies[1].wait()
    for offset, piece in enumerate(query_refs):
        size = positions // sets
        first = lax.rem(me + offset, sets) * size
        store(held_ref.at[1, pl.ds(pl.multiple_of(first, size), size)], piece)
    for slot in (0, 1):
        copies[2 + slot].wait()
        turned = held_ref[2 + slot].astype(F32).T
        turned_ref[slot] = turned.reshape(count, rows, positions).astype(BF16)
        store(turned_ref.at[slot], sent_ref.at[:, slot])
    for result in results:
        result.wait()


def heads_kernel(sets, *refs):
    parts, pieces = refs[:sets], refs[sets:]
    head_dim = pieces[0].shape[2]
    mine = lax.axis_index("seq") // sets
    for offset, piece in enumerate(pieces):
        head = lax.rem(mine + offset, len(pieces))
        lanes = pl.ds(pl.multiple_of(head * head_dim, head_dim), head_dim)
        for index, part in enumerate(parts):
            piece[index] = part[:, lanes]


def join_kernel(count, *refs):
    pieces, (joined_ref, semaphores) = refs[:count], refs[-2:]
    copies = [
        pltpu.make_async_copy(piece, joined_ref.at[index], semaphores.at[index])
        for index, piece in enumerate(pieces)
    ]
    for copy in copies:
        copy.start()
    for copy in copies:
        copy.wait()


def squares_kernel(rows, home_ref, after_ref, squares_ref):
    squares_ref[...] = jnp.sum(home_ref[:, rows:].astype(F32), axis=0)


def arrange_kernel(sets, *refs):
    key_parts, query_parts, (keys_ref, queries_ref, semaphores) = refs[:sets], refs[sets:-3], refs[-3:]
    heads = len(query_parts)
    me = lax.axis_index("seq")
    copies = []
    for index in range(heads):
        for offset in range(sets):
            source = lax.rem(me // sets + heads - index, heads) * sets + lax.rem(me + offset, sets)
            for slot, (part, target) in enumerate((
                (key_parts[offset].at[index], keys_ref.at[source]),
                (query_parts[index].at[offset], queries_ref.at[source]),
            )):
                semaphore = semaphores.at[slot, offset, index]
                copies.append(pltpu.make_async_copy(part, target, semaphore))
    for copy in copies:
        copy.start()
    for copy in copies:
        copy.wait()


def unpack_kernel(got_ref, out_ref):
    count = got_ref.shape[0]
    rows = out_ref.shape[1] // count
    whole = got_ref[:, :rows].astype(F32).reshape(count * rows, got_ref.shape[2])
    out_ref[...] = whole.T.astype(BF16)


def toeplitz_kernel(head_count_per, taps_ref, matrix_ref):
    block, length = matrix_ref.shape
    head = lax.axis_index("seq") // head_count_per
    taps = taps_ref[...].astype(F32)
    mine = lax.broadcasted_iota(jnp.int32, taps.shape, 0) == head
    row = jnp.sum(jnp.where(mine, taps, 0.0), axis=0, keepdims=True)
    rolled = pltpu.roll(jnp.broadcast_to(row, (block, length)), 0, 1, stride=1, stride_axis=0)
    source = lax.broadcasted_iota(jnp.int32, (block, block), 0)
    target = lax.broadcasted_iota(jnp.int32, (block, block), 1)
    matrix_ref[:, :block] = jnp.where(target >= source, rolled[:, :block], 0.0).astype(BF16)
    matrix_ref[:, block:] = rolled[:, block:].astype(BF16)


def conv_kernel(got_ref, matrix_ref, skip_ref, mixed_ref, back_ref, total_ref):
    count, _, rows, block = got_ref.shape
    inputs = merge_rows(got_ref[:, 0])
    before = jnp.concatenate([jnp.zeros((rows, block), BF16), inputs[: (count - 1) * rows]], axis=0)
    pairs = jnp.concatenate([inputs, before], axis=1)
    for lag in range(0, count, 2):
        spans = [slice((lag + more) * block, (lag + more + 1) * block) for more in (0, 1)]
        product = jnp.dot(
            pairs[: (count - lag) * rows],
            jnp.concatenate([matrix_ref[:, span] for span in spans], axis=0),
            preferred_element_type=F32,
        )
        if lag == 0:
            total_ref[...] = product
        else:
            total_ref[lag * rows :] += product
    skip = skip_ref[...]
    sums = []
    for index in range(count):
        conv = total_ref[index * rows : (index + 1) * rows]
        direct = skip * got_ref[index, 0].astype(F32)
        mixed = (got_ref[index, 1].astype(F32) * (conv + direct)).astype(BF16)
        mixed_ref[index] = mixed
        back_ref[index, :rows] = mixed
        widened = mixed.astype(F32)
        sums.append(jnp.sum(widened * widened, axis=0, keepdims=True))
    squares = jnp.concatenate(sums, axis=0)
    both = squares.astype(BF16)
    for index in range(count):
        back_ref[index, rows:] = both


def weights_block(step, last, key_ref, query, sets, rows, scores_ref, weights_ref, total_ref):
    wide = query.shape[0]
    seq_block = sets * rows
    reach = wide // rows * seq_block
    chunk = min(KEY_CHUNK, reach)
    chunks = (step + 1) * reach // chunk
    head_dim = query.shape[1]
    factor = math.log2(math.e) / math.sqrt(head_dim)
    mine = lax.rem(lax.axis_index("seq"), sets)
    lane = step * wide + lax.broadcasted_iota(jnp.int32, (1, wide), 1)
    query_pos = lane // rows * seq_block + mine * rows + lax.rem(lane, rows)

    def score(index, peak):
        first = index * chunk
        part = key_ref[pl.ds(first, chunk), :]
        raw = lax.dot_general(part, query, NT, preferred_element_type=F32)
        if not isinstance(index, int) or first + chunk - 1 > step * reach:
            key_pos = first + lax.broadcasted_iota(jnp.int32, (chunk, 1), 0)
            raw = jnp.where(key_pos <= query_pos, raw, -jnp.inf)
        scores_ref[pl.ds(first, chunk), :] = raw
        return jnp.maximum(peak, jnp.max(raw, axis=0, keepdims=True))

    peak = loop(chunks, score, jnp.full((1, wide), -jnp.inf, F32))

    def weigh(index, total):
        first = index * chunk
        weights = jnp.exp2((scores_ref[pl.ds(first, chunk), :] - peak) * factor)
        weights_ref[pl.ds(first, chunk), :] = weights.astype(BF16)
        return total + jnp.sum(weights, axis=0, keepdims=True)

    total = loop(chunks, weigh, jnp.zeros((1, wide), F32))
    total_ref[...] = jnp.broadcast_to(1.0 / total, total_ref.shape)


def weights_kernel(gridded, key_ref, query_ref, total_ref, *refs):
    weights_refs, scores_ref = refs[:-1], refs[-1]
    count, positions, head_dim = key_ref.shape
    rows = query_ref.shape[1]
    sets = positions // rows
    steps = count * rows // QUERY_BLOCK
    keys = key_ref.reshape(count * positions, head_dim)

    def block(step, weights, total):
        each = QUERY_BLOCK // rows
        query = merge_rows(query_ref[step * each : (step + 1) * each])
        weights_block(step, steps - 1, keys, query, sets, rows, scores_ref, weights, total)

    if not gridded:
        for step in range(steps):
            block(step, weights_refs[step], total_ref.at[step])
        return
    for step in range(steps):
        pl.when(pl.program_id(0) == step)(
            functools.partial(block, step, weights_refs[0].at[0], total_ref.at[0])
        )


def output_kernel(sets, steps, width, gridded, *refs):
    own = 4 if gridded else 6
    first = len(refs) - own - sets - (1 if gridded else steps)
    squares_refs, parts, refs = refs[:first], refs[first : first + sets], refs[first + sets :]
    total_ref, weights_refs, refs = refs[0], refs[1 : 1 - own], refs[1 - own :]
    out_ref, wide_ref, values_ref = refs[:3]
    count, rows, block = parts[0].shape
    mine = lax.rem(lax.axis_index("seq"), sets)
    reach = count * block // steps

    def norm():
        squares = sum(ref[...] for ref in squares_refs[1:]) + squares_refs[0][...]
        inv_scale = lax.rsqrt(squares / width + 1e-06)
        for offset in range(sets):
            place = lax.rem(mine + offset, sets)
            for index in range(count):
                span = slice(index * block, (index + 1) * block)
                part = parts[offset][index].astype(F32) * inv_scale[index : index + 1]
                if rows % 16:
                    wide_ref[place, :, span] = part
                else:
                    lines = pl.ds(pl.multiple_of(place * rows, rows), rows)
                    values_ref[lines, span] = part.astype(BF16)
        if rows % 16:
            for index in range(count):
                span = slice(index * block, (index + 1) * block)
                values_ref[:, span] = merge_rows(wide_ref[:, :, span]).astype(BF16)

    def attend(step, weights, total):
        keys = (step + 1) * reach
        summed = jnp.dot(values_ref[:, :keys], weights[:keys], preferred_element_type=F32)
        return (summed * total[:1]).T.astype(BF16)

    if gridded:
        pl.when(pl.program_id(0) == 0)(norm)

        def block_of(step):
            out_ref[...] = attend(step, weights_refs[0].at[0], total_ref.at[0])

        for step in range(steps):
            pl.when(pl.program_id(0) == step)(functools.partial(block_of, step))
        return
    staged_ref, semaphores = refs[3:]
    norm()
    copies = []
    for step in reversed(range(steps)):
        staged_ref[step] = attend(step, weights_refs[step], total_ref.at[step])
        lines = out_ref.at[pl.ds(step * QUERY_BLOCK, QUERY_BLOCK)]
        copies.append(pltpu.make_async_copy(staged_ref.at[step], lines, semaphores.at[step]))
        copies[-1].start()
    for copy in copies:
        copy.wait()


def shards(signal, gate_rows, skip_gain, filter_taps, queries, key_rows):
    block, local_width = signal.shape
    heads_loc = filter_taps.shape[1]
    head_dim = local_width // heads_loc
    seq_count = lax.axis_size("seq")
    chan_count = lax.axis_size("chan")
    everyone = seq_count * chan_count
    length = block * seq_count
    sets = seq_count // heads_loc
    rows = block // sets
    channels = local_width // seq_count
    query_len = length // sets
    steps = query_len // QUERY_BLOCK
    gridded = length > 4096
    shape = jax.ShapeDtypeStruct

    def from_set(array, offset):
        pairs = []
        for head in range(heads_loc):
            for part in range(sets):
                pairs.append((head * sets + (part + offset) % sets, head * sets + part))
        return lax.ppermute(array, "seq", pairs)

    def from_head(array, offset):
        pairs = [(source, (source + offset * sets) % seq_count) for source in range(seq_count)]
        return lax.ppermute(array, "seq", pairs)

    anywhere = pl.BlockSpec(memory_space=pl.ANY)
    packed, *pieces = call(
        functools.partial(pack_kernel, sets, heads_loc),
        [shape((seq_count, 2, channels, block), BF16)]
        + [shape((block, head_dim), BF16)] * heads_loc
        + [shape((rows, local_width), BF16)] * sets,
        moved=16 * signal.size,
        in_specs=[anywhere] * 4,
        out_specs=[anywhere] * (1 + heads_loc + sets),
        vmem=56,
        scratch_shapes=[
            pltpu.VMEM((4,) + signal.shape, BF16),
            pltpu.VMEM((heads_loc, block, head_dim), BF16),
            pltpu.VMEM((2, seq_count, channels, block), BF16),
            pltpu.SemaphoreType.DMA((4,)),
            pltpu.SemaphoreType.DMA((heads_loc + sets + 2,)),
        ],
    )(signal, gate_rows, queries, key_rows)
    got = lax.all_to_all(packed, "seq", 0, 0, tiled=True)
    key_pieces, set_queries = pieces[:heads_loc], pieces[heads_loc:]
    key_pieces = key_pieces[:1] + [from_head(key_pieces[k], k) for k in range(1, heads_loc)]
    matrix = call(
        functools.partial(toeplitz_kernel, sets),
        shape((block, length), BF16),
        moved=block * length * 2,
        flops=block * length * 8,
        vmem=8 if not gridded else 56,
    )(filter_taps.T)
    skip = lax.dynamic_slice_in_dim(skip_gain, lax.axis_index("seq") * channels, channels)[:, None]

    whole = pl.BlockSpec(memory_space=pltpu.VMEM)
    own_keys = call(
        functools.partial(join_kernel, heads_loc),
        shape((heads_loc, block, head_dim), BF16),
        moved=4 * signal.size,
        flops=4 * 10**10,
        in_specs=[anywhere] * (heads_loc + 1),
        out_specs=anywhere,
        scratch_shapes=[pltpu.SemaphoreType.DMA((heads_loc,))],
    )(*key_pieces, matrix)
    key_parts = [own_keys] + [from_set(own_keys, k) for k in range(1, sets)]
    query_sets = set_queries[:1] + [from_set(set_queries[-k], k) for k in range(1, sets)]
    query_pieces = call(
        functools.partial(heads_kernel, sets),
        [shape((sets, rows, head_dim), BF16)] * heads_loc,
        moved=4 * signal.size,
        flops=0,
    )(*query_sets)
    query_parts = [query_pieces[0]] + [from_head(query_pieces[k], k) for k in range(1, heads_loc)]

    mixed, back = call(
        conv_kernel,
        [
            shape((seq_count, channels, block), BF16),
            shape((seq_count, channels + seq_count, block), BF16),
        ],
        moved=signal.size * 10,
        flops=length * length * channels,
        vmem=8 if not gridded else 56,
        scratch_shapes=[pltpu.VMEM((seq_count * channels, block), F32)],
    )(got, matrix, skip)

    home = lax.all_to_all(back, "seq", 0, 0, tiled=True)
    mixed_parts = [mixed] + [from_set(mixed, offset) for offset in range(1, sets)]
    total_shape = (steps, 8, QUERY_BLOCK)
    one = lambda dims: pl.BlockSpec((1,) + dims[1:], lambda step: (step, 0, 0))
    whole = pl.BlockSpec(memory_space=pltpu.VMEM)
    if gridded:
        weights_shapes = [(steps, length, QUERY_BLOCK)]
        vmem = 56
        weights_specs = [one(total_shape), one(weights_shapes[0])]
        weights_grid = dict(grid=(steps,), in_specs=[whole] * 2, out_specs=weights_specs)
        output_grid = dict(
            grid=(steps,),
            in_specs=[whole] * (chan_count + sets) + weights_specs,
            out_specs=pl.BlockSpec((QUERY_BLOCK, head_dim), lambda step: (step, 0)),
        )
    else:
        weights_shapes = [(length * step // steps, QUERY_BLOCK) for step in range(1, steps + 1)]
        vmem = 12
        weights_grid = {}
        output_grid = dict(
            in_specs=[whole] * (chan_count + sets + 1 + steps),
            out_specs=anywhere,
        )
        output_scratch = [
            pltpu.VMEM((steps, QUERY_BLOCK, head_dim), BF16),
            pltpu.SemaphoreType.DMA((steps,)),
        ]
    keys, arranged = call(
        functools.partial(arrange_kernel, sets),
        [shape((seq_count, block, head_dim), BF16), shape((seq_count, rows, head_dim), BF16)],
        moved=6 * length * head_dim,
        flops=4 * 10**10,
        in_specs=[anywhere] * (sets + heads_loc),
        out_specs=[anywhere] * 2,
        scratch_shapes=[pltpu.SemaphoreType.DMA((2, sets, heads_loc))],
    )(*key_parts, *query_parts)
    totals, *weights = call(
        functools.partial(weights_kernel, gridded),
        [shape(total_shape, F32)] + [shape(dims, BF16) for dims in weights_shapes],
        moved=2 * sum(math.prod(dims) for dims in weights_shapes),
        flops=query_len * length * head_dim,
        exps=query_len * length // 2,
        vmem=vmem,
        scratch_shapes=[
            pltpu.VMEM((length, QUERY_BLOCK), F32),
        ],
        **weights_grid,
    )(keys, arranged)

    squares = call(
        functools.partial(squares_kernel, channels),
        shape((seq_count, block), F32),
        moved=4 * length,
        in_specs=[whole, anywhere],
        vmem=8 if not gridded else 56,
    )(home, totals)
    all_squares = [squares]
    for offset in reversed(range(1, chan_count)):
        pairs = [(source, source ^ offset) for source in range(chan_count)]
        all_squares.append(lax.ppermute(squares, "chan", pairs))

    attended = call(
        functools.partial(output_kernel, sets, steps, local_width * chan_count, gridded),
        shape((query_len, head_dim), BF16),
        moved=2 * sum(math.prod(dims) for dims in weights_shapes),
        flops=query_len * length * head_dim,
        vmem=vmem,
        scratch_shapes=[
            pltpu.VMEM((sets, channels, length if channels % 16 else block), F32),
            pltpu.VMEM((head_dim, length), BF16),
        ]
        + ([] if gridded else output_scratch),
        **output_grid,
    )(*all_squares, *mixed_parts, totals, *weights)

    conv_mixed = call(unpack_kernel, shape((block, local_width), BF16), moved=signal.size * 4)(home)
    return (conv_mixed, attended[None])


def solution(mesh):
    in_specs = (
        P("seq", "chan"),
        P("seq", "chan"),
        P("chan"),
        P(None, "chan"),
        P("seq", "chan"),
        P("seq", "chan"),
    )
    out_specs = (P("seq", "chan"), P(("chan", "seq"), None, None))
    return jax.shard_map(shards, mesh=mesh, in_specs=in_specs, out_specs=out_specs, check_vma=False)
```
